32 devices in a mesh: pairs: 8 (over z, y), aux: 4 (over x, core).
Axes of the slice: x: 2, y: 2, z: 4, core: 2. Of those that a mesh axis runs over, the one named last changes fastest.
Arguments:
- cholesky_slab: bfloat16 [2048, 35840], P('pairs', 'aux'), may hold values from -40 to 40, as said below
- test_matrix: bfloat16 [35840, 768], P('aux', 'pairs'), may hold values from -0.03125 to 0.03125
Outputs:
- projected: float32 [768, 35840], P('pairs', 'aux')
The draws below stay inside these ranges and needn't reach their ends.
Inputs may be any that keep to these rules, and one draw needn't show every extreme that they name: cholesky_slab: real entries with varying row and column magnitudes.
All inputs are finite; a program needn't handle non-finite values.
Results may differ from the reference program's by a relative error of at most 0.0003.
Values may be sent and summed in bfloat16 or wider, within the bound.
No kernel may reach another device: no remote copies, remote signals or barrier semaphores. Data moves between devices by JAX's collectives and lax.ppermute only.
A program may use at most 128 MiB of HBM per device.

```python
import math
import jax
import jax.numpy as jnp
from jax import lax

NAUX = 35840
RANK = 768
PAIRS = 2048


def draw_cholesky_slab(key, part):
    keys = jax.random.split(key, 5)
    row_scale = jnp.exp(jax.random.uniform(keys[0], (PAIRS, 1), jnp.float32, math.log(0.3), math.log(3.0)))
    col_scale = jnp.exp(jax.random.uniform(keys[1], (1, NAUX), jnp.float32, math.log(0.3), math.log(3.0)))
    base = jnp.clip(jax.random.normal(keys[4], (PAIRS, NAUX), jnp.float32), -4.0, 4.0)
    return (base * row_scale * col_scale).astype(jnp.bfloat16)


def level_of(stream_key, shape, pieces, low, largest):
    level = 1.0
    for dim, blocks in pieces:
        heights = jax.random.uniform(jax.random.fold_in(jax.random.fold_in(stream_key, 6), dim), (blocks,), jnp.float32, low / len(pieces), largest / len(pieces))
        level = level * jnp.repeat(jnp.exp(heights), shape[dim] // blocks).reshape((-1,) + (1,) * (len(shape) - 1 - dim))
    return level


def gaussian(own_key, shape, deviation, limit, pieces=(), kind=jnp.bfloat16):
    gain = level_of(own_key, shape, pieces, -0.22, 0.18) if pieces else 1.0
    array = jax.random.normal(own_key, shape, jnp.float32) * deviation * gain
    return jnp.minimum(jnp.maximum(array, -limit), limit).astype(kind)


def setup_inputs(seed: int = 0) -> dict:
    seeds = jax.random.split(jax.random.key(seed), 3)
    return {
        "cholesky_slab": draw_cholesky_slab(jax.random.fold_in(seeds[2], 71), 0),
        "test_matrix": gaussian(seeds[1], (NAUX, RANK), NAUX ** -0.5, 0.03125, ((0, 4), (1, 8))),
    }


def reference(cholesky_slab, test_matrix):
    sketch = jnp.dot(cholesky_slab.astype(jnp.float32), test_matrix.astype(jnp.float32), preferred_element_type=jnp.float32)
    gram_matrix = jnp.dot(sketch.T.astype(jnp.float32), sketch.astype(jnp.float32), precision=lax.Precision.HIGHEST, preferred_element_type=jnp.float32)
    lower_factor = jnp.linalg.cholesky(gram_matrix)
    basis_t = jax.scipy.linalg.solve_triangular(lower_factor, sketch.T, lower=True)
    projected = jnp.dot(basis_t.astype(jnp.float32), cholesky_slab.astype(basis_t.dtype).astype(jnp.float32), precision=lax.Precision.HIGHEST, preferred_element_type=jnp.float32)
    return projected
```

```python
import jax
import jax.numpy as jnp
from jax import lax
from jax.sharding import PartitionSpec as P

HIGHEST = lax.Precision.HIGHEST


def split3(x):
    hi = lax.reduce_precision(x, 8, 7)
    rest = x - hi
    mid = lax.reduce_precision(rest, 8, 7)
    return tuple(part.astype(jnp.bfloat16) for part in (hi, mid, rest - mid))


def dot_t(a, b):
    return lax.dot_general(a, b, (((0,), (0,)), ((), ())), preferred_element_type=jnp.float32)


def body(slab, test_matrix):
    n_pairs = lax.axis_size("pairs")
    slab_cols = lax.all_to_all(slab, "pairs", split_axis=1, concat_axis=0, tiled=True)
    test_rows = lax.all_to_all(test_matrix, "pairs", split_axis=0, concat_axis=1, tiled=True)
    largest = lax.pmax(jnp.max(jnp.abs(slab)).astype(jnp.float32), ("pairs", "aux"))

    partial_value = jnp.dot(slab_cols, test_rows, preferred_element_type=jnp.float32)
    rows = lax.psum_scatter(partial_value, ("pairs", "aux"), scatter_dimension=0, tiled=True)
    sketch = lax.all_gather(rows, ("pairs", "aux"), axis=0, tiled=True)

    gram = lax.dot_general(sketch, sketch, (((0,), (0,)), ((), ())), precision=HIGHEST, preferred_element_type=jnp.float32)
    hi, mid, lo = split3(sketch)
    weighted = dot_t(lo, slab_cols) + dot_t(mid, slab_cols) + dot_t(hi, slab_cols)

    factor = jnp.linalg.cholesky(gram)
    projected = jax.scipy.linalg.solve_triangular(factor, weighted, lower=True)

    all_rows = slab_cols.shape[0]
    bound = jnp.maximum(largest, 1e-30) * (all_rows ** 0.5)
    scale = 16384.0 / bound
    sent = (projected * scale).astype(jnp.float16)
    got = lax.all_to_all(sent, "pairs", split_axis=0, concat_axis=1, tiled=True)
    return got.astype(jnp.float32) * (bound / 16384.0)


def solution(mesh):
    in_specs = (P("pairs", "aux"), P("aux", "pairs"))
    out_specs = P("pairs", "aux")
    return jax.shard_map(body, mesh=mesh, in_specs=in_specs, out_specs=out_specs, check_vma=False)
```

```python
import jax
import jax.numpy as jnp
from jax import lax
from jax.experimental import pallas as pl
from jax.experimental.pallas import tpu as pltpu
from jax.sharding import PartitionSpec as P

HIGHEST = lax.Precision.HIGHEST


def split3(x):
    hi = lax.reduce_precision(x, 8, 7)
    rest = x - hi
    mid = lax.reduce_precision(rest, 8, 7)
    return tuple(part.astype(jnp.bfloat16) for part in (hi, mid, rest - mid))


def dot_t(a, b):
    return lax.dot_general(a, b, (((0,), (0,)), ((), ())), preferred_element_type=jnp.float32)


def invert_block(block):
    size = block.shape[0]
    lane = lax.broadcasted_iota(jnp.int32, (8, size), 1)
    sub = lax.broadcasted_iota(jnp.int32, (8, size), 0)

    def across(x, column):
        return jnp.broadcast_to(x[:, column : column + 1], (8, size))

    def down(x, row):
        return jnp.broadcast_to(x[row : row + 1, :], (8, size))

    slabs = [block[8 * i : 8 * i + 8, :] for i in range(size // 8)]
    for g in range(size // 8):
        base = 8 * g
        own = (lane >= base) & (lane < base + 8)
        slab = slabs[g]
        marked = jnp.where(own, jnp.where(lane == sub + base, 1.0, 0.0), slab)
        cols = [across(slab, base + j) for j in range(8)]
        d = {(i, j): down(cols[j], i) for j in range(8) for i in range(j, 8)}
        rows = [down(marked, i) for i in range(8)]
        m, recip = {}, []
        for j in range(8):
            recip.append(1.0 / d[j, j])
            for i in range(j + 1, 8):
                m[i, j] = d[i, j] * recip[j]
            for i in range(j + 1, 8):
                for k in range(j + 1, i + 1):
                    d[i, k] = d[i, k] - m[i, j] * d[k, j]
                rows[i] = rows[i] - m[i, j] * rows[j]
        solved = [rows[j] * recip[j] for j in range(8)]
        for j in range(6, -1, -1):
            for i in range(7, j, -1):
                solved[j] = solved[j] - m[i, j] * solved[i]
        for i in range(g + 1, size // 8):
            total = jnp.where(own, 0.0, slabs[i])
            for j in range(8):
                total = total - across(slabs[i], base + j) * solved[j]
            slabs[i] = total
        scaled = rows[0] * lax.rsqrt(d[0, 0])
        for j in range(1, 8):
            scaled = jnp.where(sub == j, rows[j] * lax.rsqrt(d[j, j]), scaled)
        slabs[g] = scaled
    return jnp.concatenate(slabs, axis=0)


def inverse_factor_kernel(gram_ref, out_ref, work, strip):
    size = gram_ref.shape[0]
    tile = 128
    work[...] = gram_ref[...]
    row_in = lax.broadcasted_iota(jnp.int32, (tile, tile), 0)
    col_in = lax.broadcasted_iota(jnp.int32, (tile, tile), 1)
    col = lax.broadcasted_iota(jnp.int32, (tile, size), 1)

    def step(k, carry):
        at = pl.multiple_of(k * tile, tile)
        here = pl.ds(at, tile)
        inverse = invert_block(work[here, here])
        inverse = jnp.where(row_in >= col_in, inverse, 0.0)
        work[here, here] = jnp.where(row_in == col_in, 1.0, 0.0)
        strip[...] = jnp.dot(inverse, work[here, :], precision=HIGHEST, preferred_element_type=jnp.float32)
        strip[:, here] = inverse
        out_ref[here, :] = jnp.where(col < at + tile, strip[...], 0.0)

        def below(i, carry):
            there = pl.ds(pl.multiple_of(i * tile, tile), tile)
            work[there, here] = jnp.zeros((tile, tile), jnp.float32)
            work[there, :] -= jnp.dot(strip[:, there].T, strip[...], precision=HIGHEST, preferred_element_type=jnp.float32)
            return carry

        return lax.fori_loop(k + 1, size // tile, below, carry)

    lax.fori_loop(0, size // tile, step, 0)


def inverse_factor(gram):
    size = gram.shape[0]
    return pl.pallas_call(
        inverse_factor_kernel,
        out_shape=jax.ShapeDtypeStruct((size, size), jnp.float32),
        in_specs=[pl.BlockSpec(memory_space=pltpu.VMEM)],
        out_specs=pl.BlockSpec(memory_space=pltpu.VMEM),
        scratch_shapes=[pltpu.VMEM((size, size), jnp.float32), pltpu.VMEM((128, size), jnp.float32)],
        compiler_params=pltpu.CompilerParams(vmem_limit_bytes=32 * 1024 * 1024),
        cost_estimate=pl.CostEstimate(flops=60 * size**3, bytes_accessed=8 * size**2, transcendentals=0),
    )(gram)


def body(slab, test_matrix):
    n_pairs = lax.axis_size("pairs")
    slab_cols = lax.all_to_all(slab, "pairs", split_axis=1, concat_axis=0, tiled=True)
    test_rows = lax.all_to_all(test_matrix, "pairs", split_axis=0, concat_axis=1, tiled=True)
    largest = lax.pmax(jnp.max(jnp.abs(slab)).astype(jnp.float32), ("pairs", "aux"))

    partial_value = jnp.dot(slab_cols, test_rows, preferred_element_type=jnp.float32)
    rows = lax.psum_scatter(partial_value, ("pairs", "aux"), scatter_dimension=0, tiled=True)
    sketch = lax.all_gather(rows, ("pairs", "aux"), axis=0, tiled=True)

    gram = lax.dot_general(sketch, sketch, (((0,), (0,)), ((), ())), precision=HIGHEST, preferred_element_type=jnp.float32)
    hi, mid, lo = split3(sketch)
    weighted = dot_t(lo, slab_cols) + dot_t(mid, slab_cols) + dot_t(hi, slab_cols)

    projected = jnp.dot(inverse_factor(gram), weighted, precision=HIGHEST, preferred_element_type=jnp.float32)

    all_rows = slab_cols.shape[0]
    bound = jnp.maximum(largest, 1e-30) * (all_rows ** 0.5)
    scale = 16384.0 / bound
    sent = (projected * scale).astype(jnp.float16)
    got = lax.all_to_all(sent, "pairs", split_axis=0, concat_axis=1, tiled=True)
    return got.astype(jnp.float32) * (bound / 16384.0)


def solution(mesh):
    in_specs = (P("pairs", "aux"), P("aux", "pairs"))
    out_specs = P("pairs", "aux")
    return jax.shard_map(body, mesh=mesh, in_specs=in_specs, out_specs=out_specs, check_vma=False)
```

```python
import jax
import jax.numpy as jnp
from jax import lax
from jax.experimental import pallas as pl
from jax.experimental.pallas import tpu as pltpu
from jax.sharding import PartitionSpec as P

HIGHEST = lax.Precision.HIGHEST


def split3(x):
    hi = lax.reduce_precision(x, 8, 7)
    rest = x - hi
    mid = lax.reduce_precision(rest, 8, 7)
    return tuple(part.astype(jnp.bfloat16) for part in (hi, mid, rest - mid))


def dot_t(a, b):
    return lax.dot_general(a, b, (((0,), (0,)), ((), ())), preferred_element_type=jnp.float32)


def invert_block(block):
    size = block.shape[0]
    lane = lax.broadcasted_iota(jnp.int32, (8, size), 1)
    sub = lax.broadcasted_iota(jnp.int32, (8, size), 0)

    def across(x, column):
        return jnp.broadcast_to(x[:, column : column + 1], (8, size))

    def down(x, row):
        return jnp.broadcast_to(x[row : row + 1, :], (8, size))

    slabs = [block[8 * i : 8 * i + 8, :] for i in range(size // 8)]
    for g in range(size // 8):
        base = 8 * g
        own = (lane >= base) & (lane < base + 8)
        slab = slabs[g]
        marked = jnp.where(own, jnp.where(lane == sub + base, 1.0, 0.0), slab)
        cols = [across(slab, base + j) for j in range(8)]
        d = {(i, j): down(cols[j], i) for j in range(8) for i in range(j, 8)}
        rows = [down(marked, i) for i in range(8)]
        m, recip = {}, []
        for j in range(8):
            recip.append(1.0 / d[j, j])
            for i in range(j + 1, 8):
                m[i, j] = d[i, j] * recip[j]
            for i in range(j + 1, 8):
                for k in range(j + 1, i + 1):
                    d[i, k] = d[i, k] - m[i, j] * d[k, j]
                rows[i] = rows[i] - m[i, j] * rows[j]
        solved = [rows[j] * recip[j] for j in range(8)]
        for j in range(6, -1, -1):
            for i in range(7, j, -1):
                solved[j] = solved[j] - m[i, j] * solved[i]
        for i in range(g + 1, size // 8):
            total = jnp.where(own, 0.0, slabs[i])
            for j in range(8):
                total = total - across(slabs[i], base + j) * solved[j]
            slabs[i] = total
        scaled = rows[0] * lax.rsqrt(d[0, 0])
        for j in range(1, 8):
            scaled = jnp.where(sub == j, rows[j] * lax.rsqrt(d[j, j]), scaled)
        slabs[g] = scaled
    return jnp.concatenate(slabs, axis=0)


def inverse_factor_kernel(gram_ref, out_ref, work, strip):
    size = gram_ref.shape[0]
    tile = 128
    work[...] = gram_ref[...]
    row_in = lax.broadcasted_iota(jnp.int32, (tile, tile), 0)
    col_in = lax.broadcasted_iota(jnp.int32, (tile, tile), 1)
    col = lax.broadcasted_iota(jnp.int32, (tile, size), 1)

    def step(k, carry):
        at = pl.multiple_of(k * tile, tile)
        here = pl.ds(at, tile)
        inverse = invert_block(work[here, here])
        inverse = jnp.where(row_in >= col_in, inverse, 0.0)
        work[here, here] = jnp.where(row_in == col_in, 1.0, 0.0)
        strip[...] = jnp.dot(inverse, work[here, :], precision=HIGHEST, preferred_element_type=jnp.float32)
        strip[:, here] = inverse
        out_ref[here, :] = jnp.where(col < at + tile, strip[...], 0.0)

        def below(i, carry):
            there = pl.ds(pl.multiple_of(i * tile, tile), tile)
            work[there, here] = jnp.zeros((tile, tile), jnp.float32)
            work[there, :] -= jnp.dot(strip[:, there].T, strip[...], precision=HIGHEST, preferred_element_type=jnp.float32)
            return carry

        return lax.fori_loop(k + 1, size // tile, below, carry)

    lax.fori_loop(0, size // tile, step, 0)


def inverse_factor(gram):
    size = gram.shape[0]
    return pl.pallas_call(
        inverse_factor_kernel,
        out_shape=jax.ShapeDtypeStruct((size, size), jnp.float32),
        in_specs=[pl.BlockSpec(memory_space=pltpu.VMEM)],
        out_specs=pl.BlockSpec(memory_space=pltpu.VMEM),
        scratch_shapes=[pltpu.VMEM((size, size), jnp.float32), pltpu.VMEM((128, size), jnp.float32)],
        compiler_params=pltpu.CompilerParams(vmem_limit_bytes=32 * 1024 * 1024),
        cost_estimate=pl.CostEstimate(flops=60 * size**3, bytes_accessed=8 * size**2, transcendentals=0),
    )(gram)


def rolled(x, start):
    return lax.dynamic_slice_in_dim(jnp.concatenate([x, x], axis=0), start, x.shape[0], axis=0)


def sketch_rows(slab, test_matrix):
    z, y = lax.axis_index("z"), lax.axis_index("y")
    n_z, n_y, n_aux = lax.axis_size("z"), lax.axis_size("y"), lax.axis_size("aux")
    rows, width = slab.shape[0], test_matrix.shape[1]

    up = [test_matrix.T]
    down = [up[0]]
    for s in range(1, n_z):
        up.append(lax.ppermute(up[-1], "z", [(i, i + 1) for i in range(s - 1, n_z - 1)]))
        down.append(lax.ppermute(down[-1], "z", [(i + 1, i) for i in range(n_z - s)]))
    blocks = [slab]
    for k in range(1, n_y):
        blocks.append(lax.ppermute(slab, "y", [((i + k) % n_y, i) for i in range(n_y)]))

    shards = [up[0]] + [up[s] + down[n_z - s] for s in range(1, n_z)]
    parts = [
        [
            lax.dot_general(block, shard, (((1,), (1,)), ((), ())), preferred_element_type=jnp.float32)
            for shard in shards[::-1]
        ]
        for block in blocks
    ]
    sent = jnp.stack([jnp.concatenate(p, axis=1) for p in parts])
    sent = rolled(sent, lax.rem(n_y - y, n_y)).reshape(n_y * n_aux, rows // n_aux, n_z * width)
    got = lax.all_to_all(sent, ("y", "aux"), split_axis=0, concat_axis=0, tiled=True)
    summed = got.reshape(n_y, n_aux, rows // n_aux, n_z, width).sum(axis=1)
    summed = rolled(jnp.transpose(summed, (2, 1, 0, 3)), n_z - 1 - z)
    return jnp.transpose(summed, (1, 0, 2, 3)).reshape(rows // n_aux, n_z * n_y * width)


def body(slab, test_matrix):
    largest = lax.pmax(jnp.max(jnp.abs(slab)).astype(jnp.float32), ("z", "y", "aux"))
    rows = sketch_rows(slab, test_matrix)
    slab, rows, largest = lax.optimization_barrier((slab, rows, largest))
    slab_cols = lax.all_to_all(slab, ("z", "y"), split_axis=1, concat_axis=0, tiled=True)
    sketch = lax.all_gather(rows, ("z", "y", "aux"), axis=0, tiled=True)

    gram = lax.dot_general(sketch, sketch, (((0,), (0,)), ((), ())), precision=HIGHEST, preferred_element_type=jnp.float32)
    hi, mid, lo = split3(sketch)
    weighted = dot_t(lo, slab_cols) + dot_t(mid, slab_cols) + dot_t(hi, slab_cols)

    projected = jnp.dot(inverse_factor(gram), weighted, precision=HIGHEST, preferred_element_type=jnp.float32)

    all_rows = slab_cols.shape[0]
    bound = jnp.maximum(largest, 1e-30) * (all_rows ** 0.5)
    scale = 16384.0 / bound
    sent = (projected * scale).astype(jnp.float16)
    got = lax.all_to_all(sent, ("z", "y"), split_axis=0, concat_axis=1, tiled=True)
    return got.astype(jnp.float32) * (bound / 16384.0)


def solution(mesh):
    n_pairs, n_aux = mesh.shape["pairs"], mesh.shape["aux"]
    n_y = 2 ** ((n_pairs.bit_length() - 1) // 2)
    grid = jax.sharding.Mesh(mesh.devices.reshape(n_pairs // n_y, n_y, n_aux), ("z", "y", "aux"))
    in_specs = (P(("z", "y"), "aux"), P("aux", ("z", "y")))
    out_specs = P(("z", "y"), "aux")
    return jax.shard_map(body, mesh=grid, in_specs=in_specs, out_specs=out_specs, check_vma=False)
```

```python
import jax
import jax.numpy as jnp
from jax import lax
from jax.experimental import pallas as pl
from jax.experimental.pallas import tpu as pltpu
from jax.sharding import PartitionSpec as P

HIGHEST = lax.Precision.HIGHEST


def split3(x):
    hi = lax.reduce_precision(x, 8, 7)
    rest = x - hi
    mid = lax.reduce_precision(rest, 8, 7)
    return tuple(part.astype(jnp.bfloat16) for part in (hi, mid, rest - mid))


def dot_t(a, b):
    return lax.dot_general(a, b, (((0,), (0,)), ((), ())), preferred_element_type=jnp.float32)


def invert_block(block):
    size = block.shape[0]
    lane = lax.broadcasted_iota(jnp.int32, (8, size), 1)
    sub = lax.broadcasted_iota(jnp.int32, (8, size), 0)

    def across(x, column):
        return jnp.broadcast_to(x[:, column : column + 1], (8, size))

    def down(x, row):
        return jnp.broadcast_to(x[row : row + 1, :], (8, size))

    slabs = [block[8 * i : 8 * i + 8, :] for i in range(size // 8)]
    for g in range(size // 8):
        base = 8 * g
        own = (lane >= base) & (lane < base + 8)
        slab = slabs[g]
        marked = jnp.where(own, jnp.where(lane == sub + base, 1.0, 0.0), slab)
        cols = [across(slab, base + j) for j in range(8)]
        d = {(i, j): down(cols[j], i) for j in range(8) for i in range(j, 8)}
        rows = [down(marked, i) for i in range(8)]
        m, recip = {}, []
        for j in range(8):
            recip.append(1.0 / d[j, j])
            for i in range(j + 1, 8):
                m[i, j] = d[i, j] * recip[j]
            for i in range(j + 1, 8):
                for k in range(j + 1, i + 1):
                    d[i, k] = d[i, k] - m[i, j] * d[k, j]
                rows[i] = rows[i] - m[i, j] * rows[j]
        solved = [rows[j] * recip[j] for j in range(8)]
        for j in range(6, -1, -1):
            for i in range(7, j, -1):
                solved[j] = solved[j] - m[i, j] * solved[i]
        for i in range(g + 1, size // 8):
            total = jnp.where(own, 0.0, slabs[i])
            for j in range(8):
                total = total - across(slabs[i], base + j) * solved[j]
            slabs[i] = total
        scaled = rows[0] * lax.rsqrt(d[0, 0])
        for j in range(1, 8):
            scaled = jnp.where(sub == j, rows[j] * lax.rsqrt(d[j, j]), scaled)
        slabs[g] = scaled
    return jnp.concatenate(slabs, axis=0)


def inverse_factor_kernel(gram_ref, out_ref, work, strip):
    size = gram_ref.shape[0]
    tile = 128
    work[...] = gram_ref[...]
    row_in = lax.broadcasted_iota(jnp.int32, (tile, tile), 0)
    col_in = lax.broadcasted_iota(jnp.int32, (tile, tile), 1)
    col = lax.broadcasted_iota(jnp.int32, (tile, size), 1)

    def step(k, carry):
        at = pl.multiple_of(k * tile, tile)
        here = pl.ds(at, tile)
        inverse = invert_block(work[here, here])
        inverse = jnp.where(row_in >= col_in, inverse, 0.0)
        work[here, here] = jnp.where(row_in == col_in, 1.0, 0.0)
        strip[...] = jnp.dot(inverse, work[here, :], precision=HIGHEST, preferred_element_type=jnp.float32)
        strip[:, here] = inverse
        out_ref[here, :] = jnp.where(col < at + tile, strip[...], 0.0)

        def below(i, carry):
            there = pl.ds(pl.multiple_of(i * tile, tile), tile)
            work[there, here] = jnp.zeros((tile, tile), jnp.float32)
            work[there, :] -= jnp.dot(strip[:, there].T, strip[...], precision=HIGHEST, preferred_element_type=jnp.float32)
            return carry

        return lax.fori_loop(k + 1, size // tile, below, carry)

    lax.fori_loop(0, size // tile, step, 0)


def inverse_factor(gram):
    size = gram.shape[0]
    return pl.pallas_call(
        inverse_factor_kernel,
        out_shape=jax.ShapeDtypeStruct((size, size), jnp.float32),
        in_specs=[pl.BlockSpec(memory_space=pltpu.VMEM)],
        out_specs=pl.BlockSpec(memory_space=pltpu.VMEM),
        scratch_shapes=[pltpu.VMEM((size, size), jnp.float32), pltpu.VMEM((128, size), jnp.float32)],
        compiler_params=pltpu.CompilerParams(vmem_limit_bytes=32 * 1024 * 1024),
        cost_estimate=pl.CostEstimate(flops=60 * size**3, bytes_accessed=8 * size**2, transcendentals=0),
    )(gram)


def rolled(x, start):
    return lax.dynamic_slice_in_dim(jnp.concatenate([x, x], axis=0), start, x.shape[0], axis=0)


def gathered_max(slab):
    own = jnp.full((8, 128), jnp.max(jnp.abs(slab)).astype(jnp.float32))
    return jnp.max(lax.all_gather(own, ("z", "y")))


def sketch_rows(slab, test_matrix):
    z, y = lax.axis_index("z"), lax.axis_index("y")
    n_z, n_y, n_aux = lax.axis_size("z"), lax.axis_size("y"), lax.axis_size("aux")
    rows, width = slab.shape[0], test_matrix.shape[1]

    up = [test_matrix.T]
    down = [up[0]]
    for s in range(1, n_z):
        up.append(lax.ppermute(up[-1], "z", [(i, i + 1) for i in range(s - 1, n_z - 1)]))
        down.append(lax.ppermute(down[-1], "z", [(i + 1, i) for i in range(n_z - s)]))
    blocks = [slab]
    for k in range(1, n_y):
        blocks.append(lax.ppermute(slab, "y", [((i + k) % n_y, i) for i in range(n_y)]))

    up[-1], down[-1], later, largest = lax.optimization_barrier((up[-1], down[-1], slab, gathered_max(slab)))
    slab_cols = lax.all_to_all(later, ("z", "y"), split_axis=1, concat_axis=0, tiled=True)

    shards = [up[0]] + [up[s] + down[n_z - s] for s in range(1, n_z)]
    parts = [
        [
            lax.dot_general(block, shard, (((1,), (1,)), ((), ())), preferred_element_type=jnp.float32)
            for shard in shards[::-1]
        ]
        for block in blocks
    ]
    sent = jnp.stack([jnp.concatenate(p, axis=1) for p in parts])
    sent = rolled(sent, lax.rem(n_y - y, n_y)).reshape(n_y, n_aux, rows // n_aux, n_z * width)

    aux = lax.axis_index("aux")

    def exchange(dy, da):
        piece = lax.dynamic_slice(sent, (y ^ dy, aux ^ da, 0, 0), (1, 1) + sent.shape[2:])[0, 0]
        if dy or da:
            pairs = [(i * n_aux + j, (i ^ dy) * n_aux + (j ^ da)) for i in range(n_y) for j in range(n_aux)]
            piece = lax.ppermute(piece, ("y", "aux"), pairs)
        return piece

    own_y = [sum(exchange(dy, da) for da in range(n_aux)) for dy in range(n_y)]
    summed = jnp.stack(own_y)
    summed = jnp.stack([lax.dynamic_index_in_dim(summed, y ^ k, keepdims=False) for k in range(n_y)])
    summed = jnp.transpose(summed.reshape(n_y, rows // n_aux, n_z, width), (2, 1, 0, 3))
    summed = rolled(summed, n_z - 1 - z)
    summed = jnp.transpose(summed, (1, 0, 2, 3)).reshape(rows // n_aux, n_z * n_y * width)
    return summed, slab_cols, largest


def body(slab, test_matrix):
    rows, slab_cols, largest = sketch_rows(slab, test_matrix)
    sketch = lax.all_gather(rows, ("z", "y", "aux"), axis=0, tiled=True)

    gram = lax.dot_general(sketch, sketch, (((0,), (0,)), ((), ())), precision=HIGHEST, preferred_element_type=jnp.float32)
    hi, mid, lo = split3(sketch)
    weighted = dot_t(lo, slab_cols) + dot_t(mid, slab_cols) + dot_t(hi, slab_cols)

    projected = jnp.dot(inverse_factor(gram), weighted, precision=HIGHEST, preferred_element_type=jnp.float32)

    all_rows = slab_cols.shape[0]
    bound = jnp.maximum(largest, 1e-30) * (all_rows ** 0.5)
    scale = 16384.0 / bound
    sent = (projected * scale).astype(jnp.float16)
    got = lax.all_to_all(sent, ("z", "y"), split_axis=0, concat_axis=1, tiled=True)
    return got.astype(jnp.float32) * (bound / 16384.0)


def solution(mesh):
    n_pairs, n_aux = mesh.shape["pairs"], mesh.shape["aux"]
    n_y = 2 ** ((n_pairs.bit_length() - 1) // 2)
    grid = jax.sharding.Mesh(mesh.devices.reshape(n_pairs // n_y, n_y, n_aux), ("z", "y", "aux"))
    in_specs = (P(("z", "y"), "aux"), P("aux", ("z", "y")))
    out_specs = P(("z", "y"), "aux")
    return jax.shard_map(body, mesh=grid, in_specs=in_specs, out_specs=out_specs, check_vma=False)
```

```python
import jax
import jax.numpy as jnp
from jax import lax
from jax.experimental import pallas as pl
from jax.experimental.layout import Layout, with_layout_constraint
from jax.experimental.pallas import tpu as pltpu
from jax.sharding import PartitionSpec as P

HIGHEST = lax.Precision.HIGHEST


def split3(x):
    hi = lax.reduce_precision(x, 8, 7)
    rest = x - hi
    mid = lax.reduce_precision(rest, 8, 7)
    return tuple(part.astype(jnp.bfloat16) for part in (hi, mid, rest - mid))


def dot_t(a, b):
    return lax.dot_general(a, b, (((0,), (0,)), ((), ())), preferred_element_type=jnp.float32)


def invert_block(block):
    size = block.shape[0]
    lane = lax.broadcasted_iota(jnp.int32, (8, size), 1)
    sub = lax.broadcasted_iota(jnp.int32, (8, size), 0)

    def across(x, column):
        return jnp.broadcast_to(x[:, column : column + 1], (8, size))

    def down(x, row):
        return jnp.broadcast_to(x[row : row + 1, :], (8, size))

    slabs = [block[8 * i : 8 * i + 8, :] for i in range(size // 8)]
    for g in range(size // 8):
        base = 8 * g
        own = (lane >= base) & (lane < base + 8)
        slab = slabs[g]
        marked = jnp.where(own, jnp.where(lane == sub + base, 1.0, 0.0), slab)
        cols = [across(slab, base + j) for j in range(8)]
        d = {(i, j): down(cols[j], i) for j in range(8) for i in range(j, 8)}
        rows = [down(marked, i) for i in range(8)]
        m, recip = {}, []
        for j in range(8):
            recip.append(1.0 / d[j, j])
            for i in range(j + 1, 8):
                m[i, j] = d[i, j] * recip[j]
            for i in range(j + 1, 8):
                for k in range(j + 1, i + 1):
                    d[i, k] = d[i, k] - m[i, j] * d[k, j]
                rows[i] = rows[i] - m[i, j] * rows[j]
        solved = [rows[j] * recip[j] for j in range(8)]
        for j in range(6, -1, -1):
            for i in range(7, j, -1):
                solved[j] = solved[j] - m[i, j] * solved[i]
        for i in range(g + 1, size // 8):
            total = jnp.where(own, 0.0, slabs[i])
            for j in range(8):
                total = total - across(slabs[i], base + j) * solved[j]
            slabs[i] = total
        scaled = rows[0] * lax.rsqrt(d[0, 0])
        for j in range(1, 8):
            scaled = jnp.where(sub == j, rows[j] * lax.rsqrt(d[j, j]), scaled)
        slabs[g] = scaled
    return jnp.concatenate(slabs, axis=0)


def inverse_factor_kernel(gram_ref, out_ref, work, strip):
    size = gram_ref.shape[0]
    tile = 128
    work[...] = gram_ref[...]
    row_in = lax.broadcasted_iota(jnp.int32, (tile, tile), 0)
    col_in = lax.broadcasted_iota(jnp.int32, (tile, tile), 1)
    col = lax.broadcasted_iota(jnp.int32, (tile, size), 1)

    def step(k, carry):
        at = pl.multiple_of(k * tile, tile)
        here = pl.ds(at, tile)
        inverse = invert_block(work[here, here])
        inverse = jnp.where(row_in >= col_in, inverse, 0.0)
        work[here, here] = jnp.where(row_in == col_in, 1.0, 0.0)
        strip[...] = jnp.dot(inverse, work[here, :], precision=HIGHEST, preferred_element_type=jnp.float32)
        strip[:, here] = inverse
        out_ref[here, :] = jnp.where(col < at + tile, strip[...], 0.0)

        def below(i, carry):
            there = pl.ds(pl.multiple_of(i * tile, tile), tile)
            work[there, here] = jnp.zeros((tile, tile), jnp.float32)
            work[there, :] -= jnp.dot(strip[:, there].T, strip[...], precision=HIGHEST, preferred_element_type=jnp.float32)
            return carry

        return lax.fori_loop(k + 1, size // tile, below, carry)

    lax.fori_loop(0, size // tile, step, 0)


def inverse_factor(gram):
    size = gram.shape[0]
    return pl.pallas_call(
        inverse_factor_kernel,
        out_shape=jax.ShapeDtypeStruct((size, size), jnp.float32),
        in_specs=[pl.BlockSpec(memory_space=pltpu.VMEM)],
        out_specs=pl.BlockSpec(memory_space=pltpu.VMEM),
        scratch_shapes=[pltpu.VMEM((size, size), jnp.float32), pltpu.VMEM((128, size), jnp.float32)],
        compiler_params=pltpu.CompilerParams(vmem_limit_bytes=32 * 1024 * 1024),
        cost_estimate=pl.CostEstimate(flops=60 * size**3, bytes_accessed=8 * size**2, transcendentals=0),
    )(gram)


def rolled(x, start):
    return lax.dynamic_slice_in_dim(jnp.concatenate([x, x], axis=0), start, x.shape[0], axis=0)


def row_major(x):
    return with_layout_constraint(x, Layout(major_to_minor=tuple(range(x.ndim))))


def tie(*arrays):
    return lax.optimization_barrier(arrays)


def body(slab, test_matrix):
    z, y, aux = lax.axis_index("z"), lax.axis_index("y"), lax.axis_index("aux")
    n_z, n_y, n_aux = lax.axis_size("z"), lax.axis_size("y"), lax.axis_size("aux")
    rows, width = slab.shape[0], test_matrix.shape[1]
    n_cols = slab.shape[1] // (n_z * n_y)

    up = [test_matrix.T]
    down = [up[0]]
    blocks = [row_major(slab.T)]
    for k in range(1, n_y):
        blocks.append(lax.ppermute(blocks[0], "y", [((i + k) % n_y, i) for i in range(n_y)]))

    def piece(to_z):
        start = (to_z * n_y + y) * n_cols
        return jnp.stack([lax.dynamic_slice(b, (start, 0), (n_cols, rows)) for b in blocks])

    def send(d, firsts):
        ups = [(i, i + d) for i in firsts]
        downs = [(n_z - 1 - i, n_z - 1 - j) for i, j in ups]
        return [(d, lax.ppermute(above[d], "z", ups)), (n_z - d, lax.ppermute(below[d], "z", downs))]

    for s in range(1, n_z):
        if s == n_z - 1:
            above = {d: piece(z + d) for d in range(1, n_z)}
            below = {d: piece(z - d) for d in range(1, n_z)}
            above[1], below[1], up[-1], down[-1] = tie(above[1], below[1], up[-1], down[-1])
            moved = send(1, range(n_z - 2))
        up.append(lax.ppermute(up[-1], "z", [(i, i + 1) for i in range(s - 1, n_z - 1)]))
        down.append(lax.ppermute(down[-1], "z", [(i + 1, i) for i in range(n_z - s)]))

    above[1], below[1], above[2], below[2], up[-1], down[-1] = tie(above[1], below[1], above[2], below[2], up[-1], down[-1])
    second = send(1, [n_z - 2]) + send(2, [0])

    shards = [up[0]] + [up[s] + down[n_z - s] for s in range(1, n_z)]
    sent = jnp.stack(
        [
            jnp.concatenate([jnp.dot(shard, block, preferred_element_type=jnp.float32) for shard in shards[::-1]], axis=0).T
            for block in blocks
        ]
    )
    sent = rolled(sent, lax.rem(n_y - y, n_y)).reshape(n_y, n_aux, rows // n_aux, n_z * width)

    def exchange(dy, da):
        part = lax.dynamic_slice(sent, (y ^ dy, aux ^ da, 0, 0), (1, 1) + sent.shape[2:])[0, 0]
        if dy or da:
            pairs = [(i * n_aux + j, (i ^ dy) * n_aux + (j ^ da)) for i in range(n_y) for j in range(n_aux)]
            part = lax.ppermute(part, ("y", "aux"), pairs)
        return part

    summed = jnp.stack([sum(exchange(dy, da) for da in range(n_aux)) for dy in range(n_y)])
    summed = jnp.stack([lax.dynamic_index_in_dim(summed, y ^ k, keepdims=False) for k in range(n_y)])
    summed = jnp.transpose(summed.reshape(n_y, rows // n_aux, n_z, width), (2, 1, 0, 3))
    summed = rolled(summed, n_z - 1 - z)
    own_rows = jnp.transpose(summed, (1, 0, 2, 3)).reshape(rows // n_aux, n_z * n_y * width)

    tied = tie(own_rows, *[x for _, x in second])
    moved += [(s, x) for (s, _), x in zip(second, tied[1:])]
    sketch = lax.all_gather(tied[0], ("z", "y", "aux"), axis=0, tiled=True)

    names = [d for d in range(2, n_z)]
    tied = tie(sketch, *[above[d] for d in names], *[below[d] for d in names])
    sketch = tied[0]
    above = dict(zip(names, tied[1:]))
    below = dict(zip(names, tied[1 + len(names) :]))
    third = []
    for d in names:
        firsts = range(1 if d == 2 else 0, n_z - d)
        if len(firsts):
            third += send(d, firsts)

    gram = lax.dot_general(sketch, sketch, (((0,), (0,)), ((), ())), precision=HIGHEST, preferred_element_type=jnp.float32)
    tied = tie(inverse_factor(gram), sketch, *[x for _, x in third])
    inverse, sketch = tied[:2]
    moved += [(s, x) for (s, _), x in zip(third, tied[2:])]

    arrived = [piece(z)] + [sum(x for t, x in moved if t == s) for s in range(1, n_z)]
    arrived = rolled(jnp.stack(arrived[::-1]), n_z - 1 - z)
    arrived = rolled(jnp.swapaxes(arrived, 0, 1), lax.rem(n_y - y, n_y))
    slab_cols = jnp.transpose(arrived, (2, 1, 0, 3)).reshape(n_cols, n_z * n_y * rows)

    weighted = sum(jnp.dot(slab_cols, part, preferred_element_type=jnp.float32) for part in split3(sketch)[::-1])
    projected = lax.dot_general(
        inverse, weighted, (((1,), (1,)), ((), ())), precision=HIGHEST, preferred_element_type=jnp.float32
    )

    largest = jnp.maximum(jnp.max(jnp.abs(projected)), 1e-30)
    power = jnp.floor(14.0 - jnp.log2(largest))
    n_more = 128 - n_cols % 128
    more = jnp.broadcast_to(power.astype(jnp.float16), (projected.shape[0], n_more))
    packed = jnp.concatenate([(projected * jnp.exp2(power)).astype(jnp.float16), more], axis=1)
    packed = packed.reshape(n_z * n_y, -1, n_cols + n_more)
    got = lax.all_to_all(packed, ("z", "y"), split_axis=0, concat_axis=0, tiled=True).astype(jnp.float32)
    got = got[:, :, :n_cols] * jnp.exp2(-got[:, :1, n_cols : n_cols + 1])
    return jnp.transpose(got, (1, 0, 2)).reshape(got.shape[1], -1)


def solution(mesh):
    n_pairs, n_aux = mesh.shape["pairs"], mesh.shape["aux"]
    n_y = 2 ** ((n_pairs.bit_length() - 1) // 2)
    grid = jax.sharding.Mesh(mesh.devices.reshape(n_pairs // n_y, n_y, n_aux), ("z", "y", "aux"))
    in_specs = (P(("z", "y"), "aux"), P("aux", ("z", "y")))
    out_specs = P(("z", "y"), "aux")
    return jax.shard_map(body, mesh=grid, in_specs=in_specs, out_specs=out_specs, check_vma=False)
```

```python
import jax
import jax.numpy as jnp
from jax import lax
from jax.experimental import pallas as pl
from jax.experimental.layout import Layout, with_layout_constraint
from jax.experimental.pallas import tpu as pltpu
from jax.sharding import PartitionSpec as P

HIGHEST = lax.Precision.HIGHEST


def invert_block(block):
    size = block.shape[0]
    lane = lax.broadcasted_iota(jnp.int32, (8, size), 1)
    sub = lax.broadcasted_iota(jnp.int32, (8, size), 0)

    def across(x, column):
        return jnp.broadcast_to(x[:, column : column + 1], (8, size))

    def down(x, row):
        return jnp.broadcast_to(x[row : row + 1, :], (8, size))

    slabs = [block[8 * i : 8 * i + 8, :] for i in range(size // 8)]
    for g in range(size // 8):
        base = 8 * g
        own = (lane >= base) & (lane < base + 8)
        slab = slabs[g]
        marked = jnp.where(own, jnp.where(lane == sub + base, 1.0, 0.0), slab)
        cols = [across(slab, base + j) for j in range(8)]
        d = {(i, j): down(cols[j], i) for j in range(8) for i in range(j, 8)}
        rows = [down(marked, i) for i in range(8)]
        m, recip = {}, []
        for j in range(8):
            recip.append(1.0 / d[j, j])
            for i in range(j + 1, 8):
                m[i, j] = d[i, j] * recip[j]
            for i in range(j + 1, 8):
                for k in range(j + 1, i + 1):
                    d[i, k] = d[i, k] - m[i, j] * d[k, j]
                rows[i] = rows[i] - m[i, j] * rows[j]
        solved = [rows[j] * recip[j] for j in range(8)]
        for j in range(6, -1, -1):
            for i in range(7, j, -1):
                solved[j] = solved[j] - m[i, j] * solved[i]
        for i in range(g + 1, size // 8):
            total = jnp.where(own, 0.0, slabs[i])
            for j in range(8):
                total = total - across(slabs[i], base + j) * solved[j]
            slabs[i] = total
        scaled = rows[0] * lax.rsqrt(d[0, 0])
        for j in range(1, 8):
            scaled = jnp.where(sub == j, rows[j] * lax.rsqrt(d[j, j]), scaled)
        slabs[g] = scaled
    return jnp.concatenate(slabs, axis=0)


def inverse_factor_kernel(*refs):
    *strips, out_ref, work, strip = refs
    size = out_ref.shape[0]
    tile = 128
    top = 0
    for ref in strips:
        work[top : top + ref.shape[0], top:] = ref[...]
        top += ref.shape[0]
    row_in = lax.broadcasted_iota(jnp.int32, (tile, tile), 0)
    col_in = lax.broadcasted_iota(jnp.int32, (tile, tile), 1)
    col = lax.broadcasted_iota(jnp.int32, (tile, size), 1)

    def step(k, carry):
        at = pl.multiple_of(k * tile, tile)
        here = pl.ds(at, tile)
        inverse = invert_block(work[here, here])
        inverse = jnp.where(row_in >= col_in, inverse, 0.0)
        work[here, here] = jnp.where(row_in == col_in, 1.0, 0.0)
        strip[...] = jnp.dot(inverse, work[here, :], precision=HIGHEST, preferred_element_type=jnp.float32)
        strip[:, here] = inverse
        out_ref[here, :] = jnp.where(col < at + tile, strip[...], 0.0)

        def below(i, carry):
            there = pl.ds(pl.multiple_of(i * tile, tile), tile)
            work[there, here] = jnp.zeros((tile, tile), jnp.float32)
            work[there, :] -= jnp.dot(strip[:, there].T, strip[...], precision=HIGHEST, preferred_element_type=jnp.float32)
            return carry

        return lax.fori_loop(k + 1, size // tile, below, carry)

    lax.fori_loop(0, size // tile, step, 0)


def inverse_factor(strips):
    size = strips[0].shape[1]
    return pl.pallas_call(
        inverse_factor_kernel,
        out_shape=jax.ShapeDtypeStruct((size, size), jnp.float32),
        in_specs=[pl.BlockSpec(memory_space=pltpu.VMEM)] * len(strips),
        out_specs=pl.BlockSpec(memory_space=pltpu.VMEM),
        scratch_shapes=[pltpu.VMEM((size, size), jnp.float32), pltpu.VMEM((128, size), jnp.float32)],
        compiler_params=pltpu.CompilerParams(vmem_limit_bytes=32 * 1024 * 1024),
        cost_estimate=pl.CostEstimate(flops=2 * size**3, bytes_accessed=8 * size**2, transcendentals=0),
    )(*strips)


def project_kernel(order_ref, sketch_ref, inverse_ref, *refs):
    *pieces, out_ref, slab_cols, high, middle, weighted, product = refs
    n_y, n_cols, rows = pieces[0].shape
    padded = weighted.shape[0]
    n_rank = sketch_ref.shape[1]
    tile = high.shape[1]

    for k, piece in enumerate(pieces):
        for j in range(n_y):
            at = pl.multiple_of(order_ref[k * n_y + j] * rows, rows)
            slab_cols[:n_cols, pl.ds(at, rows)] = piece[j]
    if padded > n_cols:
        weighted[n_cols:, :] = jnp.zeros((padded - n_cols, n_rank), jnp.float32)

    def weigh(j, carry):
        at = pl.ds(pl.multiple_of(j * tile, tile), tile)
        part = sketch_ref[:, at]
        high[...] = part.astype(jnp.bfloat16)
        middle[...] = (part - high[...].astype(jnp.float32)).astype(jnp.bfloat16)
        total = jnp.dot(slab_cols[...], middle[...], preferred_element_type=jnp.float32)
        total += jnp.dot(slab_cols[...], high[...], preferred_element_type=jnp.float32)
        weighted[:n_cols, at] = total
        return carry

    lax.fori_loop(0, n_rank // tile, weigh, 0)

    largest = jnp.full((1, 1), 1e-30, jnp.float32)
    for top in range(0, n_rank, tile):
        upto = top + tile
        value = lax.dot_general(
            inverse_ref[top:upto, :upto],
            weighted[:, :upto],
            (((1,), (1,)), ((), ())),
            precision=HIGHEST,
            preferred_element_type=jnp.float32,
        )
        product[top:upto, :] = value
        largest = jnp.maximum(largest, jnp.max(jnp.abs(value), keepdims=True))

    power = jnp.floor(14.0 - jnp.log2(largest))
    scale = jnp.exp2(power)
    col = lax.broadcasted_iota(jnp.int32, (tile, padded), 1)
    for top in range(0, n_rank, tile):
        value = jnp.where(col < n_cols, product[top : top + tile, :] * scale, power)
        out_ref[top : top + tile, :] = value.astype(out_ref.dtype)


def project(order, sketch, inverse, pieces):
    n_y, n_cols, rows = pieces[0].shape
    all_rows, n_rank = sketch.shape
    padded = (n_cols // 128 + 1) * 128
    tile = 256
    flops = 2 * n_cols * n_rank * (2 * all_rows + 4 * n_rank)
    return pl.pallas_call(
        project_kernel,
        out_shape=jax.ShapeDtypeStruct((n_rank, padded), jnp.float32),
        in_specs=[pl.BlockSpec(memory_space=pltpu.SMEM)] + [pl.BlockSpec(memory_space=pltpu.VMEM)] * (2 + len(pieces)),
        out_specs=pl.BlockSpec(memory_space=pltpu.VMEM),
        scratch_shapes=[
            pltpu.VMEM((n_cols, all_rows), jnp.bfloat16),
            pltpu.VMEM((all_rows, tile), jnp.bfloat16),
            pltpu.VMEM((all_rows, tile), jnp.bfloat16),
            pltpu.VMEM((padded, n_rank), jnp.float32),
            pltpu.VMEM((n_rank, padded), jnp.float32),
        ],
        compiler_params=pltpu.CompilerParams(vmem_limit_bytes=56 * 1024 * 1024),
        cost_estimate=pl.CostEstimate(flops=flops, bytes_accessed=16 * 1024 * 1024, transcendentals=0),
    )(order, sketch, inverse, *pieces)


def rolled(x, start):
    return lax.dynamic_slice_in_dim(jnp.concatenate([x, x], axis=0), start, x.shape[0], axis=0)


def row_major(x):
    return with_layout_constraint(x, Layout(major_to_minor=tuple(range(x.ndim))))


def tie(*arrays):
    return lax.optimization_barrier(arrays)


def routes(n):
    if n == 4:
        return [[2, 0, 3, 1], [1, 3, 0, 2], [3, 2, 1, 0]]
    return [[(i + d) % n for i in range(n)] for d in range(1, n)]


def body(slab, test_matrix):
    z, y, aux = lax.axis_index("z"), lax.axis_index("y"), lax.axis_index("aux")
    n_z, n_y, n_aux = lax.axis_size("z"), lax.axis_size("y"), lax.axis_size("aux")
    rows, width = slab.shape[0], test_matrix.shape[1]
    n_cols = slab.shape[1] // (n_z * n_y)

    blocks = [slab] + [
        lax.ppermute(slab, "y", [((i + k) % n_y, i) for i in range(n_y)]) for k in range(1, n_y)
    ]
    up = [test_matrix.T]
    down = [up[0]]
    for s in range(1, n_z):
        up.append(lax.ppermute(up[-1], "z", [(i, i + 1) for i in range(s - 1, n_z - 1)]))
        down.append(lax.ppermute(down[-1], "z", [(i + 1, i) for i in range(n_z - s)]))
    shards = [(z, up[0])]
    for s in range(1, n_z):
        if 2 * s < n_z:
            shards += [(z - s, up[s]), (z + s, down[s])]
        else:
            shards.append((jnp.where(z >= s, z - s, z + s), up[s] + down[s]))

    def shard_sum(block):
        total = 0.0
        for place, shard in shards:
            part = lax.dot_general(block, shard, (((1,), (1,)), ((), ())), preferred_element_type=jnp.float32)
            total += jnp.concatenate([jnp.where(place == i, part, 0.0) for i in range(n_z)], axis=1)
        return total

    sent = jnp.stack([shard_sum(block) for block in blocks])
    sent = rolled(sent, lax.rem(n_y - y, n_y)).reshape(n_y, n_aux, rows // n_aux, n_z * width)

    turned = [row_major(block.T) for block in blocks]

    def piece(to_z):
        start = (to_z * n_y + y) * n_cols
        return jnp.stack([lax.dynamic_slice(b, (start, 0), (n_cols, rows)) for b in turned])

    def route(places, value):
        return lax.ppermute(value, "z", list(enumerate(places)))

    ways = routes(n_z)
    outgoing = [piece(jnp.asarray(places)[z]) for places in ways]
    tied = tie(up[-1], down[-1], *outgoing)
    incoming = [route(places, value) for places, value in zip(ways[:2], tied[2:])]

    def exchange(dy, da):
        part = lax.dynamic_slice(sent, (y ^ dy, aux ^ da, 0, 0), (1, 1) + sent.shape[2:])[0, 0]
        if dy or da:
            pairs = [(i * n_aux + j, (i ^ dy) * n_aux + (j ^ da)) for i in range(n_y) for j in range(n_aux)]
            part = lax.ppermute(part, ("y", "aux"), pairs)
        return part

    summed = jnp.stack([sum(exchange(dy, da) for da in range(n_aux)) for dy in range(n_y)])
    summed = jnp.stack([lax.dynamic_index_in_dim(summed, y ^ k, keepdims=False) for k in range(n_y)])
    summed = jnp.transpose(summed.reshape(n_y, rows // n_aux, n_z, width), (1, 2, 0, 3))
    own_rows = summed.reshape(rows // n_aux, n_z * n_y * width)

    own_rows, incoming[0] = tie(own_rows, incoming[0])
    sketch = lax.all_gather(own_rows, ("z", "y", "aux"), axis=0, tiled=True)

    tied = tie(sketch, incoming[1], *outgoing[2:])
    sketch, incoming[1] = tied[:2]
    incoming += [route(places, value) for places, value in zip(ways[2:], tied[2:])]

    strips = [
        lax.dot_general(
            sketch[:, at : at + 256],
            sketch[:, at:],
            (((0,), (0,)), ((), ())),
            precision=HIGHEST,
            preferred_element_type=jnp.float32,
        )
        for at in range(0, sketch.shape[1], 256)
    ]
    tied = tie(inverse_factor(strips), sketch, *incoming)

    from_z = [z] + [jnp.asarray([places.index(i) for i in range(n_z)])[z] for places in ways]
    order = jnp.stack([f * n_y + lax.rem(y + k, n_y) for f in from_z for k in range(n_y)]).astype(jnp.int32)
    packed = project(order, tied[1], tied[0], [piece(z), *tied[2:]])
    packed = packed.astype(jnp.float16).reshape(n_z * n_y, -1, packed.shape[1])
    got = lax.all_to_all(packed, ("z", "y"), split_axis=0, concat_axis=0, tiled=True).astype(jnp.float32)
    got = got[:, :, :n_cols] * jnp.exp2(-got[:, :1, n_cols : n_cols + 1])
    return jnp.transpose(got, (1, 0, 2)).reshape(got.shape[1], -1)


def solution(mesh):
    n_pairs, n_aux = mesh.shape["pairs"], mesh.shape["aux"]
    n_y = 2 ** ((n_pairs.bit_length() - 1) // 2)
    grid = jax.sharding.Mesh(mesh.devices.reshape(n_pairs // n_y, n_y, n_aux), ("z", "y", "aux"))
    in_specs = (P(("z", "y"), "aux"), P("aux", ("z", "y")))
    out_specs = P(("z", "y"), "aux")
    return jax.shard_map(body, mesh=grid, in_specs=in_specs, out_specs=out_specs, check_vma=False)
```

```python
import jax
import jax.numpy as jnp
from jax import lax
from jax.experimental import pallas as pl
from jax.experimental.layout import Layout, with_layout_constraint
from jax.experimental.pallas import tpu as pltpu
from jax.sharding import PartitionSpec as P

HIGHEST = lax.Precision.HIGHEST


def invert_block(block):
    size = block.shape[0]
    lane = lax.broadcasted_iota(jnp.int32, (8, size), 1)
    sub = lax.broadcasted_iota(jnp.int32, (8, size), 0)

    def across(x, column):
        return jnp.broadcast_to(x[:, column : column + 1], (8, size))

    def down(x, row):
        return jnp.broadcast_to(x[row : row + 1, :], (8, size))

    slabs = [block[8 * i : 8 * i + 8, :] for i in range(size // 8)]
    for g in range(size // 8):
        base = 8 * g
        own = (lane >= base) & (lane < base + 8)
        slab = slabs[g]
        marked = jnp.where(own, jnp.where(lane == sub + base, 1.0, 0.0), slab)
        cols = [across(slab, base + j) for j in range(8)]
        d = {(i, j): down(cols[j], i) for j in range(8) for i in range(j, 8)}
        rows = [down(marked, i) for i in range(8)]
        m, recip = {}, []
        for j in range(8):
            recip.append(1.0 / d[j, j])
            for i in range(j + 1, 8):
                m[i, j] = d[i, j] * recip[j]
            for i in range(j + 1, 8):
                for k in range(j + 1, i + 1):
                    d[i, k] = d[i, k] - m[i, j] * d[k, j]
                rows[i] = rows[i] - m[i, j] * rows[j]
        solved = [rows[j] * recip[j] for j in range(8)]
        for j in range(6, -1, -1):
            for i in range(7, j, -1):
                solved[j] = solved[j] - m[i, j] * solved[i]
        for i in range(g + 1, size // 8):
            total = jnp.where(own, 0.0, slabs[i])
            for j in range(7, -1, -1):
                total = total - across(slabs[i], base + j) * solved[j]
            slabs[i] = total
        scaled = rows[0] * lax.rsqrt(d[0, 0])
        for j in range(1, 8):
            scaled = jnp.where(sub == j, rows[j] * lax.rsqrt(d[j, j]), scaled)
        slabs[g] = scaled
    return jnp.concatenate(slabs, axis=0)


def eliminate(work, out_ref, strip):
    size = work.shape[0]
    tile = 128
    row_in = lax.broadcasted_iota(jnp.int32, (tile, tile), 0)
    col_in = lax.broadcasted_iota(jnp.int32, (tile, tile), 1)
    col = lax.broadcasted_iota(jnp.int32, (tile, size), 1)

    def step(k, carry):
        at = pl.multiple_of(k * tile, tile)
        here = pl.ds(at, tile)
        inverse = invert_block(work[here, here])
        inverse = jnp.where(row_in >= col_in, inverse, 0.0)
        work[here, here] = jnp.where(row_in == col_in, 1.0, 0.0)
        strip[...] = jnp.dot(inverse, work[here, :], precision=HIGHEST, preferred_element_type=jnp.float32)
        strip[:, here] = inverse
        out_ref[here, :] = jnp.where(col < at + tile, strip[...], 0.0)

        def below(i, carry):
            there = pl.ds(pl.multiple_of(i * tile, tile), tile)
            work[there, here] = jnp.zeros((tile, tile), jnp.float32)
            work[there, :] -= jnp.dot(strip[:, there].T, strip[...], precision=HIGHEST, preferred_element_type=jnp.float32)
            return carry

        return lax.fori_loop(k + 1, size // tile, below, carry)

    lax.fori_loop(0, size // tile, step, 0)


def first_factor_kernel(gram_ref, out_ref, work, strip):
    work[...] = gram_ref[...]
    eliminate(work, out_ref, strip)


def second_factor_kernel(first_ref, cross_ref, gram_ref, out_ref, work, strip, second):
    half = gram_ref.shape[0]

    def times(a, b):
        return jnp.dot(a, b, precision=HIGHEST, preferred_element_type=jnp.float32)

    first = first_ref[...]
    upper = times(first, cross_ref[...])
    lower = upper.T
    work[...] = gram_ref[...] - times(lower, upper)
    out_ref[:half, :half] = first
    out_ref[:half, half:] = jnp.zeros((half, half), jnp.float32)
    out_ref[half:, :half] = times(lower, first)
    eliminate(work, second, strip)
    out_ref[half:, half:] = second[...]
    out_ref[half:, :half] = -times(second[...], out_ref[half:, :half])


def factor_call(kernel, size, args, n_scratch):
    half = args[0].shape[0]
    square = pltpu.VMEM((half, half), jnp.float32)
    return pl.pallas_call(
        kernel,
        out_shape=jax.ShapeDtypeStruct((size, size), jnp.float32),
        in_specs=[pl.BlockSpec(memory_space=pltpu.VMEM)] * len(args),
        out_specs=pl.BlockSpec(memory_space=pltpu.VMEM),
        scratch_shapes=[square, pltpu.VMEM((128, half), jnp.float32)] + [square] * n_scratch,
        compiler_params=pltpu.CompilerParams(vmem_limit_bytes=24 * 1024 * 1024),
        cost_estimate=pl.CostEstimate(flops=2 * half**3, bytes_accessed=8 * half**2, transcendentals=0),
    )(*args)


def dot_nt(a, b):
    return lax.dot_general(a, b, (((1,), (1,)), ((), ())), preferred_element_type=jnp.float32)


def two_parts(x):
    high = x.astype(jnp.bfloat16)
    return high, (x - high.astype(jnp.float32)).astype(jnp.bfloat16)


def project_kernel(order_ref, first_ref, second_ref, inverse_ref, *refs):
    *pieces, out_ref, slab_cols, high, middle, w_high, w_middle, product = refs
    n_y, n_cols, rows = pieces[0].shape
    n_rank, padded = product.shape
    half = first_ref.shape[1]
    tile = high.shape[1]

    for k, piece in enumerate(pieces):
        for j in range(n_y):
            at = pl.multiple_of(order_ref[k * n_y + j] * rows, rows)
            slab_cols[:n_cols, pl.ds(at, rows)] = piece[j]
    if padded > n_cols:
        w_high[n_cols:, :] = jnp.zeros((padded - n_cols, n_rank), jnp.bfloat16)
        w_middle[n_cols:, :] = jnp.zeros((padded - n_cols, n_rank), jnp.bfloat16)

    for top in range(0, n_rank, tile):
        for at in range(top, top + tile, 128):
            ref, start = (first_ref, at) if at < half else (second_ref, at - half)
            parts = two_parts(ref[:, start : start + 128])
            high[:, at - top : at - top + 128], middle[:, at - top : at - top + 128] = parts
        total = jnp.dot(slab_cols[...], middle[...], preferred_element_type=jnp.float32)
        total += jnp.dot(slab_cols[...], high[...], preferred_element_type=jnp.float32)
        w_high[:n_cols, top : top + tile], w_middle[:n_cols, top : top + tile] = two_parts(total)

    largest = jnp.full((1, 1), 1e-30, jnp.float32)
    for top in range(0, n_rank, tile):
        upto = top + tile
        i_high, i_middle = two_parts(inverse_ref[top:upto, :upto])
        value = dot_nt(i_middle, w_high[:, :upto]) + dot_nt(i_high, w_middle[:, :upto])
        value += dot_nt(i_high, w_high[:, :upto])
        product[top:upto, :] = value
        largest = jnp.maximum(largest, jnp.max(jnp.abs(value), keepdims=True))

    power = jnp.floor(14.0 - jnp.log2(largest))
    scale = jnp.exp2(power)
    col = lax.broadcasted_iota(jnp.int32, (tile, padded), 1)
    for top in range(0, n_rank, tile):
        out_ref[top : top + tile, :] = jnp.where(col < n_cols, product[top : top + tile, :] * scale, power)


def project(order, first, second, inverse, pieces):
    n_y, n_cols, rows = pieces[0].shape
    all_rows, n_rank = first.shape[0], inverse.shape[0]
    padded = (n_cols // 128 + 1) * 128
    tile = 256
    flops = 2 * n_cols * n_rank * (2 * all_rows + 2 * n_rank)
    return pl.pallas_call(
        project_kernel,
        out_shape=jax.ShapeDtypeStruct((n_rank, padded), jnp.float32),
        in_specs=[pl.BlockSpec(memory_space=pltpu.SMEM)] + [pl.BlockSpec(memory_space=pltpu.VMEM)] * (3 + len(pieces)),
        out_specs=pl.BlockSpec(memory_space=pltpu.VMEM),
        scratch_shapes=[
            pltpu.VMEM((n_cols, all_rows), jnp.bfloat16),
            pltpu.VMEM((all_rows, tile), jnp.bfloat16),
            pltpu.VMEM((all_rows, tile), jnp.bfloat16),
            pltpu.VMEM((padded, n_rank), jnp.bfloat16),
            pltpu.VMEM((padded, n_rank), jnp.bfloat16),
            pltpu.VMEM((n_rank, padded), jnp.float32),
        ],
        compiler_params=pltpu.CompilerParams(vmem_limit_bytes=56 * 1024 * 1024),
        cost_estimate=pl.CostEstimate(flops=flops, bytes_accessed=16 * 1024 * 1024, transcendentals=0),
    )(order, first, second, inverse, *pieces)


def rolled(x, start):
    return lax.dynamic_slice_in_dim(jnp.concatenate([x, x], axis=0), start, x.shape[0], axis=0)


def row_major(x):
    return with_layout_constraint(x, Layout(major_to_minor=tuple(range(x.ndim))))


def tie(*arrays):
    return lax.optimization_barrier(arrays)


def routes(n):
    if n == 4:
        return [[2, 0, 3, 1], [1, 3, 0, 2], [3, 2, 1, 0]]
    return [[(i + d) % n for i in range(n)] for d in range(1, n)]


def body(slab, test_matrix):
    z, y, aux = lax.axis_index("z"), lax.axis_index("y"), lax.axis_index("aux")
    n_z, n_y, n_aux = lax.axis_size("z"), lax.axis_size("y"), lax.axis_size("aux")
    rows, width = slab.shape[0], test_matrix.shape[1]
    n_cols = slab.shape[1] // (n_z * n_y)

    blocks = [slab] + [
        row_major(lax.ppermute(slab, "y", [((i + k) % n_y, i) for i in range(n_y)])) for k in range(1, n_y)
    ]
    up = [test_matrix.T]
    down = [up[0]]
    for s in range(1, n_z):
        up.append(lax.ppermute(up[-1], "z", [(i, i + 1) for i in range(s - 1, n_z - 1)]))
        down.append(lax.ppermute(down[-1], "z", [(i + 1, i) for i in range(n_z - s)]))
    shards = [(z, up[0])]
    for s in range(1, n_z):
        if 2 * s < n_z:
            shards += [(z - s, up[s]), (z + s, down[s])]
        else:
            shards.append((jnp.where(z >= s, z - s, z + s), up[s] + down[s]))

    def shard_sum(block):
        total = 0.0
        for place, shard in shards:
            part = lax.dot_general(block, shard, (((1,), (1,)), ((), ())), preferred_element_type=jnp.float32)
            total += jnp.concatenate([jnp.where(place == i, part, 0.0) for i in range(n_z)], axis=1)
        return total

    sent = jnp.stack([shard_sum(block) for block in blocks])
    sent = rolled(sent, lax.rem(n_y - y, n_y)).reshape(n_y, n_aux, rows // n_aux, n_z * width)

    turned = [row_major(block.T) for block in blocks]

    def piece(to_z):
        start = (to_z * n_y + y) * n_cols
        return jnp.stack([lax.dynamic_slice(b, (start, 0), (n_cols, rows)) for b in turned])

    def route(places, value):
        return lax.ppermute(value, "z", list(enumerate(places)))

    ways = routes(n_z)
    outgoing = [piece(jnp.asarray(places)[z]) for places in ways]
    tied = tie(up[-1], down[-1], *outgoing)
    incoming = [route(places, value) for places, value in zip(ways[:2], tied[2:])]

    def exchange(dy, da):
        part = lax.dynamic_slice(sent, (y ^ dy, aux ^ da, 0, 0), (1, 1) + sent.shape[2:])[0, 0]
        if dy or da:
            pairs = [(i * n_aux + j, (i ^ dy) * n_aux + (j ^ da)) for i in range(n_y) for j in range(n_aux)]
            part = lax.ppermute(part, ("y", "aux"), pairs)
        return part

    summed = jnp.stack([sum(exchange(dy, da) for da in range(n_aux)) for dy in range(n_y)])
    summed = jnp.stack([lax.dynamic_index_in_dim(summed, y ^ k, keepdims=False) for k in range(n_y)])
    summed = jnp.transpose(summed.reshape(n_y, rows // n_aux, n_z, width), (1, 2, 0, 3))
    own_rows = summed.reshape(rows // n_aux, n_z * n_y * width)

    own_rows, incoming[0] = tie(own_rows, incoming[0])
    half = own_rows.shape[1] // 2
    first = lax.all_gather(own_rows[:, :half], ("z", "y", "aux"), axis=0, tiled=True)
    second = lax.all_gather(own_rows[:, half:], ("z", "y", "aux"), axis=0, tiled=True)

    tied = tie(first, incoming[1], *outgoing[2:])
    first, incoming[1] = tied[:2]
    incoming += [route(places, value) for places, value in zip(ways[2:], tied[2:])]

    def gram(a, b):
        return lax.dot_general(a, b, (((0,), (0,)), ((), ())), precision=HIGHEST, preferred_element_type=jnp.float32)

    leading = factor_call(first_factor_kernel, half, [gram(first, first)], 0)
    inverse = factor_call(second_factor_kernel, 2 * half, [leading, gram(first, second), gram(second, second)], 1)
    inverse, first, second, *incoming = tie(inverse, first, second, *incoming)

    from_z = [z] + [jnp.asarray([places.index(i) for i in range(n_z)])[z] for places in ways]
    order = jnp.stack([f * n_y + lax.rem(y + k, n_y) for f in from_z for k in range(n_y)]).astype(jnp.int32)
    packed = project(order, first, second, inverse, [piece(z), *incoming])
    packed = packed.astype(jnp.float16).reshape(n_z * n_y, -1, packed.shape[1])
    got = lax.all_to_all(packed, ("z", "y"), split_axis=0, concat_axis=0, tiled=True).astype(jnp.float32)
    got = got[:, :, :n_cols] * jnp.exp2(-got[:, :1, n_cols : n_cols + 1])
    return jnp.transpose(got, (1, 0, 2)).reshape(got.shape[1], -1)


def solution(mesh):
    n_pairs, n_aux = mesh.shape["pairs"], mesh.shape["aux"]
    n_y = 2 ** ((n_pairs.bit_length() - 1) // 2)
    grid = jax.sharding.Mesh(mesh.devices.reshape(n_pairs // n_y, n_y, n_aux), ("z", "y", "aux"))
    in_specs = (P(("z", "y"), "aux"), P("aux", ("z", "y")))
    out_specs = P(("z", "y"), "aux")
    return jax.shard_map(body, mesh=grid, in_specs=in_specs, out_specs=out_specs, check_vma=False)
```

```python
import jax
import jax.numpy as jnp
from jax import lax
from jax.experimental import pallas as pl
from jax.experimental.layout import Layout, with_layout_constraint
from jax.experimental.pallas import tpu as pltpu
from jax.sharding import PartitionSpec as P

HIGHEST = lax.Precision.HIGHEST


def invert_block(block):
    size = block.shape[0]
    lane = lax.broadcasted_iota(jnp.int32, (8, size), 1)
    sub = lax.broadcasted_iota(jnp.int32, (8, size), 0)

    def across(x, column):
        return jnp.broadcast_to(x[:, column : column + 1], (8, size))

    def down(x, row):
        return jnp.broadcast_to(x[row : row + 1, :], (8, size))

    slabs = [block[8 * i : 8 * i + 8, :] for i in range(size // 8)]
    for g in range(size // 8):
        base = 8 * g
        own = (lane >= base) & (lane < base + 8)
        slab = slabs[g]
        marked = jnp.where(own, jnp.where(lane == sub + base, 1.0, 0.0), slab)
        cols = [across(slab, base + j) for j in range(8)]
        d = {(i, j): down(cols[j], i) for j in range(8) for i in range(j, 8)}
        rows = [down(marked, i) for i in range(8)]
        m, recip = {}, []
        for j in range(8):
            recip.append(1.0 / d[j, j])
            for i in range(j + 1, 8):
                m[i, j] = d[i, j] * recip[j]
            for i in range(j + 1, 8):
                for k in range(j + 1, i + 1):
                    d[i, k] = d[i, k] - m[i, j] * d[k, j]
                rows[i] = rows[i] - m[i, j] * rows[j]
        solved = [rows[j] * recip[j] for j in range(8)]
        for j in range(6, -1, -1):
            for i in range(7, j, -1):
                solved[j] = solved[j] - m[i, j] * solved[i]
        for i in range(g + 1, size // 8):
            total = jnp.where(own, 0.0, slabs[i])
            for j in range(7, -1, -1):
                total = total - across(slabs[i], base + j) * solved[j]
            slabs[i] = total
        scaled = rows[0] * lax.rsqrt(d[0, 0])
        for j in range(1, 8):
            scaled = jnp.where(sub == j, rows[j] * lax.rsqrt(d[j, j]), scaled)
        slabs[g] = scaled
    return jnp.concatenate(slabs, axis=0)


def eliminate(work, out_ref, strip):
    size = work.shape[0]
    tile = 128
    row_in = lax.broadcasted_iota(jnp.int32, (tile, tile), 0)
    col_in = lax.broadcasted_iota(jnp.int32, (tile, tile), 1)
    col = lax.broadcasted_iota(jnp.int32, (tile, size), 1)

    def step(k, carry):
        at = pl.multiple_of(k * tile, tile)
        here = pl.ds(at, tile)
        inverse = invert_block(work[here, here])
        inverse = jnp.where(row_in >= col_in, inverse, 0.0)
        work[here, here] = jnp.where(row_in == col_in, 1.0, 0.0)
        strip[...] = jnp.dot(inverse, work[here, :], precision=HIGHEST, preferred_element_type=jnp.float32)
        strip[:, here] = inverse
        out_ref[here, :] = jnp.where(col < at + tile, strip[...], 0.0)

        def below(i, carry):
            there = pl.ds(pl.multiple_of(i * tile, tile), tile)
            work[there, here] = jnp.zeros((tile, tile), jnp.float32)
            work[there, :] -= jnp.dot(strip[:, there].T, strip[...], precision=HIGHEST, preferred_element_type=jnp.float32)
            return carry

        return lax.fori_loop(k + 1, size // tile, below, carry)

    lax.fori_loop(0, size // tile, step, 0)


def inverse_factor_kernel(own_ref, other_ref, out_ref, work, strip):
    work[...] = own_ref[...] + other_ref[...]
    eliminate(work, out_ref, strip)


def inverse_factor(own, other):
    size = own.shape[0]
    return pl.pallas_call(
        inverse_factor_kernel,
        out_shape=jax.ShapeDtypeStruct((size, size), jnp.float32),
        in_specs=[pl.BlockSpec(memory_space=pltpu.VMEM)] * 2,
        out_specs=pl.BlockSpec(memory_space=pltpu.VMEM),
        scratch_shapes=[pltpu.VMEM((size, size), jnp.float32), pltpu.VMEM((128, size), jnp.float32)],
        compiler_params=pltpu.CompilerParams(vmem_limit_bytes=24 * 1024 * 1024),
        cost_estimate=pl.CostEstimate(flops=2 * size**3, bytes_accessed=8 * size**2, transcendentals=0),
    )(own, other)


def dot_nt(a, b):
    return lax.dot_general(a, b, (((1,), (1,)), ((), ())), preferred_element_type=jnp.float32)


def two_parts(x):
    high = x.astype(jnp.bfloat16)
    return high, (x - high.astype(jnp.float32)).astype(jnp.bfloat16)


def project_kernel(order_ref, own_ref, other_ref, inverse_ref, *refs):
    *pieces, out_ref, slab_cols, high, middle, w_high, w_middle, product = refs
    n_y, n_cols, rows = pieces[0].shape
    n_rank, padded = product.shape
    n_own = own_ref.shape[0]
    tile = high.shape[1]
    half = rows // 2

    core = order_ref[0]
    for k, piece in enumerate(pieces):
        for j in range(n_y):
            at = order_ref[1 + k * n_y + j] * half
            for side, base in ((core, 0), (1 - core, n_own)):
                lanes = pl.ds(pl.multiple_of(side * half, half), half)
                slab_cols[:n_cols, pl.ds(pl.multiple_of(at + base, half), half)] = piece[j, :, lanes]
    if padded > n_cols:
        w_high[n_cols:, :] = jnp.zeros((padded - n_cols, n_rank), jnp.bfloat16)
        w_middle[n_cols:, :] = jnp.zeros((padded - n_cols, n_rank), jnp.bfloat16)

    for top in range(0, n_rank, tile):
        for ref, base in ((own_ref, 0), (other_ref, n_own)):
            parts = two_parts(ref[:, top : top + tile])
            high[base : base + n_own, :], middle[base : base + n_own, :] = parts
        total = jnp.dot(slab_cols[...], middle[...], preferred_element_type=jnp.float32)
        total += jnp.dot(slab_cols[...], high[...], preferred_element_type=jnp.float32)
        w_high[:n_cols, top : top + tile], w_middle[:n_cols, top : top + tile] = two_parts(total)

    largest = jnp.full((1, 1), 1e-30, jnp.float32)
    for top in range(0, n_rank, tile):
        upto = top + tile
        i_high, i_middle = two_parts(inverse_ref[top:upto, :upto])
        value = dot_nt(i_middle, w_high[:, :upto]) + dot_nt(i_high, w_middle[:, :upto])
        value += dot_nt(i_high, w_high[:, :upto])
        product[top:upto, :] = value
        largest = jnp.maximum(largest, jnp.max(jnp.abs(value), keepdims=True))

    power = jnp.floor(14.0 - jnp.log2(largest))
    scale = jnp.exp2(power)
    col = lax.broadcasted_iota(jnp.int32, (tile, padded), 1)
    for top in range(0, n_rank, tile):
        out_ref[top : top + tile, :] = jnp.where(col < n_cols, product[top : top + tile, :] * scale, power)


def project(order, own, other, inverse, pieces):
    n_y, n_cols, rows = pieces[0].shape
    all_rows, n_rank = 2 * own.shape[0], inverse.shape[0]
    padded = (n_cols // 128 + 1) * 128
    tile = 256
    scratch = [
        ((n_cols, all_rows), jnp.bfloat16),
        ((all_rows, tile), jnp.bfloat16),
        ((all_rows, tile), jnp.bfloat16),
        ((padded, n_rank), jnp.bfloat16),
        ((padded, n_rank), jnp.bfloat16),
        ((n_rank, padded), jnp.float32),
    ]
    held = sum(x.size * x.dtype.itemsize for x in (own, other, inverse, *pieces)) + 4 * n_rank * padded
    held += sum(x[0] * x[1] * jnp.dtype(kind).itemsize for x, kind in scratch)
    return pl.pallas_call(
        project_kernel,
        out_shape=jax.ShapeDtypeStruct((n_rank, padded), jnp.float32),
        in_specs=[pl.BlockSpec(memory_space=pltpu.SMEM)] + [pl.BlockSpec(memory_space=pltpu.VMEM)] * (3 + len(pieces)),
        out_specs=pl.BlockSpec(memory_space=pltpu.VMEM),
        scratch_shapes=[pltpu.VMEM(*x) for x in scratch],
        compiler_params=pltpu.CompilerParams(vmem_limit_bytes=held + 8 * 1024 * 1024),
        cost_estimate=pl.CostEstimate(
            flops=2 * n_cols * n_rank * (2 * all_rows + 2 * n_rank), bytes_accessed=16 * 1024 * 1024, transcendentals=0
        ),
    )(order, own, other, inverse, *pieces)


def rolled(x, start):
    return lax.dynamic_slice_in_dim(jnp.concatenate([x, x], axis=0), start, x.shape[0], axis=0)


def row_major(x):
    return with_layout_constraint(x, Layout(major_to_minor=tuple(range(x.ndim))))


def tie(*arrays):
    return lax.optimization_barrier(arrays)


def routes(n):
    if n == 4:
        return [[2, 0, 3, 1], [1, 3, 0, 2], [3, 2, 1, 0]]
    return [[(i + d) % n for i in range(n)] for d in range(1, n)]


def body(slab, test_matrix):
    z, y, x, core = (lax.axis_index(name) for name in ("z", "y", "x", "core"))
    n_z, n_y, n_x, n_core = (lax.axis_size(name) for name in ("z", "y", "x", "core"))
    n_aux = n_x * n_core
    rows, width = slab.shape[0], test_matrix.shape[1]
    n_cols = slab.shape[1] // (n_z * n_y)

    blocks = [slab] + [
        row_major(lax.ppermute(slab, "y", [((i + k) % n_y, i) for i in range(n_y)])) for k in range(1, n_y)
    ]
    up = [test_matrix.T]
    down = [up[0]]
    for s in range(1, n_z):
        up.append(lax.ppermute(up[-1], "z", [(i, i + 1) for i in range(s - 1, n_z - 1)]))
        down.append(lax.ppermute(down[-1], "z", [(i + 1, i) for i in range(n_z - s)]))
    shards = [(z, up[0])]
    for s in range(1, n_z):
        if 2 * s < n_z:
            shards += [(z - s, up[s]), (z + s, down[s])]
        else:
            shards.append((jnp.where(z >= s, z - s, z + s), up[s] + down[s]))

    turned = [row_major(block.T) for block in blocks]

    def shard_sum(block):
        total = 0.0
        for place, shard in shards:
            part = jnp.dot(shard, block, preferred_element_type=jnp.float32)
            total += jnp.concatenate([jnp.where(place == i, part, 0.0) for i in range(n_z)], axis=0)
        return total.T

    sent = jnp.stack([shard_sum(block) for block in turned])
    sent = rolled(sent, lax.rem(n_y - y, n_y)).reshape(n_y, n_core, n_x, rows // n_aux, n_z * width)

    def piece(to_z):
        start = (to_z * n_y + y) * n_cols
        return jnp.stack([lax.dynamic_slice(b, (start, 0), (n_cols, rows)) for b in turned])

    def route(places, value):
        return lax.ppermute(value, "z", list(enumerate(places)))

    ways = routes(n_z)
    outgoing = [piece(jnp.asarray(places)[z]) for places in ways]
    outgoing[0], up[-1], down[-1] = tie(outgoing[0], up[-1], down[-1])
    incoming = [route(ways[0], outgoing[0])]

    def exchange(dy, dx, dc):
        part = lax.dynamic_slice(sent, (y ^ dy, core ^ dc, x ^ dx, 0, 0), (1, 1, 1) + sent.shape[3:])[0, 0, 0]
        if dy or dx or dc:
            places = [(i, j, k) for i in range(n_y) for j in range(n_x) for k in range(n_core)]
            pairs = [(n, places.index((i ^ dy, j ^ dx, k ^ dc))) for n, (i, j, k) in enumerate(places)]
            part = lax.ppermute(part, ("y", "x", "core"), pairs)
        return part

    summed = jnp.stack([sum(exchange(dy, dx, dc) for dx in range(n_x) for dc in range(n_core)) for dy in range(n_y)])
    summed = jnp.stack([lax.dynamic_index_in_dim(summed, y ^ k, keepdims=False) for k in range(n_y)])
    summed = jnp.transpose(summed.reshape(n_y, rows // n_aux, n_z, width), (1, 2, 0, 3))
    own_rows = summed.reshape(rows // n_aux, n_z * n_y * width)

    own_rows, incoming[0] = tie(own_rows, incoming[0])
    own = lax.all_gather(own_rows, ("z", "y", "x"), axis=0, tiled=True)
    other = lax.ppermute(own, "core", [(i, n_core - 1 - i) for i in range(n_core)])

    tied = tie(own, *outgoing[1:])
    own = tied[0]
    incoming += [route(places, value) for places, value in zip(ways[1:], tied[1:])]

    def gram(a):
        return lax.dot_general(a, a, (((0,), (0,)), ((), ())), precision=HIGHEST, preferred_element_type=jnp.float32)

    inverse = inverse_factor(gram(own), gram(other))
    inverse, own, other, *incoming = tie(inverse, own, other, *incoming)

    from_z = [z] + [jnp.asarray([places.index(i) for i in range(n_z)])[z] for places in ways]
    order = jnp.stack([core] + [f * n_y + lax.rem(y + k, n_y) for f in from_z for k in range(n_y)]).astype(jnp.int32)
    packed = project(order, own, other, inverse, [piece(z), *incoming])
    packed = packed.astype(jnp.float16).reshape(n_z * n_y, -1, packed.shape[1])
    got = lax.all_to_all(packed, ("z", "y"), split_axis=0, concat_axis=0, tiled=True).astype(jnp.float32)
    got = got[:, :, :n_cols] * jnp.exp2(-got[:, :1, n_cols : n_cols + 1])
    return jnp.transpose(got, (1, 0, 2)).reshape(got.shape[1], -1)


def solution(mesh):
    n_pairs, n_aux = mesh.shape["pairs"], mesh.shape["aux"]
    n_y = 2 ** ((n_pairs.bit_length() - 1) // 2)
    shape = (n_pairs // n_y, n_y, n_aux // 2, 2)
    grid = jax.sharding.Mesh(mesh.devices.reshape(shape), ("z", "y", "x", "core"))
    in_specs = (P(("z", "y"), ("x", "core")), P(("x", "core"), ("z", "y")))
    out_specs = P(("z", "y"), ("x", "core"))
    return jax.shard_map(body, mesh=grid, in_specs=in_specs, out_specs=out_specs, check_vma=False)
```

```python
import jax
import jax.numpy as jnp
from jax import lax
from jax.experimental import pallas as pl
from jax.experimental.layout import Layout, with_layout_constraint
from jax.experimental.pallas import tpu as pltpu
from jax.sharding import PartitionSpec as P

HIGHEST = lax.Precision.HIGHEST


def invert_block(block):
    size = block.shape[0]
    lane = lax.broadcasted_iota(jnp.int32, (8, size), 1)
    sub = lax.broadcasted_iota(jnp.int32, (8, size), 0)

    def across(x, column):
        return jnp.broadcast_to(x[:, column : column + 1], (8, size))

    def down(x, row):
        return jnp.broadcast_to(x[row : row + 1, :], (8, size))

    slabs = [block[8 * i : 8 * i + 8, :] for i in range(size // 8)]
    for g in range(size // 8):
        base = 8 * g
        own = (lane >= base) & (lane < base + 8)
        slab = slabs[g]
        marked = jnp.where(own, jnp.where(lane == sub + base, 1.0, 0.0), slab)
        cols = [across(slab, base + j) for j in range(8)]
        d = {(i, j): down(cols[j], i) for j in range(8) for i in range(j, 8)}
        rows = [down(marked, i) for i in range(8)]
        m, recip = {}, []
        for j in range(8):
            guess = pl.reciprocal(d[j, j], approx=True)
            guess = guess * (2.0 - d[j, j] * guess)
            recip.append(guess * (2.0 - d[j, j] * guess))
            for i in range(j + 1, 8):
                m[i, j] = d[i, j] * recip[j]
            for i in range(j + 1, 8):
                for k in range(j + 1, i + 1):
                    d[i, k] = d[i, k] - m[i, j] * d[k, j]
                rows[i] = rows[i] - m[i, j] * rows[j]
        solved = [rows[j] * recip[j] for j in range(8)]
        for j in range(6, -1, -1):
            for i in range(7, j, -1):
                solved[j] = solved[j] - m[i, j] * solved[i]
        for i in range(g + 1, size // 8):
            total = jnp.where(own, 0.0, slabs[i])
            for j in range(7, -1, -1):
                total = total - across(slabs[i], base + j) * solved[j]
            slabs[i] = total
        scaled = rows[0] * lax.rsqrt(d[0, 0])
        for j in range(1, 8):
            scaled = jnp.where(sub == j, rows[j] * lax.rsqrt(d[j, j]), scaled)
        slabs[g] = scaled
    return jnp.concatenate(slabs, axis=0)


def eliminate(work, out_ref, strip):
    size = work.shape[0]
    tile = 128
    row_in = lax.broadcasted_iota(jnp.int32, (tile, tile), 0)
    col_in = lax.broadcasted_iota(jnp.int32, (tile, tile), 1)
    col = lax.broadcasted_iota(jnp.int32, (tile, size), 1)

    def step(k, carry):
        at = pl.multiple_of(k * tile, tile)
        here = pl.ds(at, tile)
        inverse = invert_block(work[here, here])
        inverse = jnp.where(row_in >= col_in, inverse, 0.0)
        work[here, here] = jnp.where(row_in == col_in, 1.0, 0.0)
        strip[...] = jnp.dot(inverse, work[here, :], precision=HIGHEST, preferred_element_type=jnp.float32)
        strip[:, here] = inverse
        out_ref[here, :] = jnp.where(col < at + tile, strip[...], 0.0)

        def below(i, carry):
            there = pl.ds(pl.multiple_of(i * tile, tile), tile)
            work[there, here] = jnp.zeros((tile, tile), jnp.float32)
            work[there, :] -= jnp.dot(strip[:, there].T, strip[...], precision=HIGHEST, preferred_element_type=jnp.float32)
            return carry

        return lax.fori_loop(k + 1, size // tile, below, carry)

    lax.fori_loop(0, size // tile, step, 0)


def inverse_factor_kernel(own_ref, other_ref, out_ref, work, strip):
    work[...] = own_ref[...] + other_ref[...]
    eliminate(work, out_ref, strip)


def inverse_factor(own, other):
    size = own.shape[0]
    return pl.pallas_call(
        inverse_factor_kernel,
        out_shape=jax.ShapeDtypeStruct((size, size), jnp.float32),
        in_specs=[pl.BlockSpec(memory_space=pltpu.VMEM)] * 2,
        out_specs=pl.BlockSpec(memory_space=pltpu.VMEM),
        scratch_shapes=[pltpu.VMEM((size, size), jnp.float32), pltpu.VMEM((128, size), jnp.float32)],
        compiler_params=pltpu.CompilerParams(vmem_limit_bytes=24 * 1024 * 1024),
        cost_estimate=pl.CostEstimate(flops=2 * size**3, bytes_accessed=8 * size**2, transcendentals=0),
    )(own, other)


def dot_nt(a, b):
    return lax.dot_general(a, b, (((1,), (1,)), ((), ())), preferred_element_type=jnp.float32)


def two_parts(x):
    high = x.astype(jnp.bfloat16)
    return high, (x - high.astype(jnp.float32)).astype(jnp.bfloat16)


def project_kernel(order_ref, own_ref, other_ref, inverse_ref, *refs):
    *pieces, out_ref, slab_cols, high, middle, w_high, w_middle, product = refs
    n_y, n_cols, rows = pieces[0].shape
    n_rank, padded = product.shape
    n_own = own_ref.shape[0]
    tile = high.shape[1]
    half = rows // 2

    core = order_ref[0]
    for k, piece in enumerate(pieces):
        for j in range(n_y):
            at = order_ref[1 + k * n_y + j] * half
            for side, base in ((core, 0), (1 - core, n_own)):
                lanes = pl.ds(pl.multiple_of(side * half, half), half)
                slab_cols[:n_cols, pl.ds(pl.multiple_of(at + base, half), half)] = piece[j, :, lanes]
    if padded > n_cols:
        w_high[n_cols:, :] = jnp.zeros((padded - n_cols, n_rank), jnp.bfloat16)
        w_middle[n_cols:, :] = jnp.zeros((padded - n_cols, n_rank), jnp.bfloat16)

    for top in range(0, n_rank, tile):
        for ref, base in ((own_ref, 0), (other_ref, n_own)):
            parts = two_parts(ref[:, top : top + tile])
            high[base : base + n_own, :], middle[base : base + n_own, :] = parts
        total = jnp.dot(slab_cols[...], middle[...], preferred_element_type=jnp.float32)
        total += jnp.dot(slab_cols[...], high[...], preferred_element_type=jnp.float32)
        w_high[:n_cols, top : top + tile], w_middle[:n_cols, top : top + tile] = two_parts(total)

    largest = jnp.full((1, 1), 1e-30, jnp.float32)
    for top in range(0, n_rank, tile):
        upto = top + tile
        i_high, i_middle = two_parts(inverse_ref[top:upto, :upto])
        value = dot_nt(i_middle, w_high[:, :upto]) + dot_nt(i_high, w_middle[:, :upto])
        value += dot_nt(i_high, w_high[:, :upto])
        product[top:upto, :] = value
        largest = jnp.maximum(largest, jnp.max(jnp.abs(value), keepdims=True))

    power = jnp.floor(14.0 - jnp.log2(largest))
    scale = jnp.exp2(power)
    col = lax.broadcasted_iota(jnp.int32, (tile, padded), 1)
    for top in range(0, n_rank, tile):
        out_ref[top : top + tile, :] = jnp.where(col < n_cols, product[top : top + tile, :] * scale, power)


def project(order, own, other, inverse, pieces):
    n_y, n_cols, rows = pieces[0].shape
    all_rows, n_rank = 2 * own.shape[0], inverse.shape[0]
    padded = (n_cols // 128 + 1) * 128
    tile = 256
    scratch = [
        ((n_cols, all_rows), jnp.bfloat16),
        ((all_rows, tile), jnp.bfloat16),
        ((all_rows, tile), jnp.bfloat16),
        ((padded, n_rank), jnp.bfloat16),
        ((padded, n_rank), jnp.bfloat16),
        ((n_rank, padded), jnp.float32),
    ]
    held = sum(x.size * x.dtype.itemsize for x in (own, other, inverse, *pieces)) + 4 * n_rank * padded
    held += sum(x[0] * x[1] * jnp.dtype(kind).itemsize for x, kind in scratch)
    return pl.pallas_call(
        project_kernel,
        out_shape=jax.ShapeDtypeStruct((n_rank, padded), jnp.float32),
        in_specs=[pl.BlockSpec(memory_space=pltpu.SMEM)] + [pl.BlockSpec(memory_space=pltpu.VMEM)] * (3 + len(pieces)),
        out_specs=pl.BlockSpec(memory_space=pltpu.VMEM),
        scratch_shapes=[pltpu.VMEM(*x) for x in scratch],
        compiler_params=pltpu.CompilerParams(vmem_limit_bytes=held + 8 * 1024 * 1024),
        cost_estimate=pl.CostEstimate(
            flops=2 * n_cols * n_rank * (2 * all_rows + 2 * n_rank), bytes_accessed=16 * 1024 * 1024, transcendentals=0
        ),
    )(order, own, other, inverse, *pieces)


def rolled(x, start):
    return lax.dynamic_slice_in_dim(jnp.concatenate([x, x], axis=0), start, x.shape[0], axis=0)


def row_major(x):
    return with_layout_constraint(x, Layout(major_to_minor=tuple(range(x.ndim))))


def tie(*arrays):
    return lax.optimization_barrier(arrays)


def routes(n):
    if n == 4:
        return [[2, 0, 3, 1], [1, 3, 0, 2], [3, 2, 1, 0]]
    return [[(i + d) % n for i in range(n)] for d in range(1, n)]


def body(slab, test_matrix):
    z, y, x, core = (lax.axis_index(name) for name in ("z", "y", "x", "core"))
    n_z, n_y, n_x, n_core = (lax.axis_size(name) for name in ("z", "y", "x", "core"))
    n_aux = n_x * n_core
    rows, width = slab.shape[0], test_matrix.shape[1]
    n_cols = slab.shape[1] // (n_z * n_y)

    blocks = [slab] + [
        row_major(lax.ppermute(slab, "y", [((i + k) % n_y, i) for i in range(n_y)])) for k in range(1, n_y)
    ]
    up = [test_matrix.T]
    down = [up[0]]
    for s in range(1, n_z):
        up.append(lax.ppermute(up[-1], "z", [(i, i + 1) for i in range(s - 1, n_z - 1)]))
        down.append(lax.ppermute(down[-1], "z", [(i + 1, i) for i in range(n_z - s)]))
    shards = [(z, up[0])]
    for s in range(1, n_z):
        if 2 * s < n_z:
            shards += [(z - s, up[s]), (z + s, down[s])]
        else:
            shards.append((jnp.where(z >= s, z - s, z + s), up[s] + down[s]))

    turned = [row_major(block.T) for block in blocks]

    def shard_sum(block):
        total = 0.0
        for place, shard in shards:
            part = jnp.dot(shard, block, preferred_element_type=jnp.float32)
            total += jnp.concatenate([jnp.where(place == i, part, 0.0) for i in range(n_z)], axis=0)
        return total.T

    sent = jnp.stack([shard_sum(block) for block in turned])
    sent = rolled(sent, lax.rem(n_y - y, n_y)).reshape(n_y, n_core, n_x, rows // n_aux, n_z * width)

    def piece(to_z):
        start = (to_z * n_y + y) * n_cols
        return jnp.stack([lax.dynamic_slice(b, (start, 0), (n_cols, rows)) for b in turned])

    def route(places, value):
        return lax.ppermute(value, "z", list(enumerate(places)))

    ways = routes(n_z)
    outgoing = [piece(jnp.asarray(places)[z]) for places in ways]
    incoming = [route(places, value) for places, value in zip(ways[:2], outgoing)]

    def exchange(dy, dx, dc):
        part = lax.dynamic_slice(sent, (y ^ dy, core ^ dc, x ^ dx, 0, 0), (1, 1, 1) + sent.shape[3:])[0, 0, 0]
        if dy or dx or dc:
            places = [(i, j, k) for i in range(n_y) for j in range(n_x) for k in range(n_core)]
            pairs = [(n, places.index((i ^ dy, j ^ dx, k ^ dc))) for n, (i, j, k) in enumerate(places)]
            part = lax.ppermute(part, ("y", "x", "core"), pairs)
        return part

    summed = jnp.stack([sum(exchange(dy, dx, dc) for dx in range(n_x) for dc in range(n_core)) for dy in range(n_y)])
    summed = jnp.stack([lax.dynamic_index_in_dim(summed, y ^ k, keepdims=False) for k in range(n_y)])
    summed = jnp.transpose(summed.reshape(n_y, rows // n_aux, n_z, width), (1, 2, 0, 3))
    own_rows = summed.reshape(rows // n_aux, n_z * n_y * width)

    own_rows, incoming[0] = tie(own_rows, incoming[0])
    own = lax.all_gather(own_rows, ("z", "y", "x"), axis=0, tiled=True)
    other = lax.ppermute(own, "core", [(i, n_core - 1 - i) for i in range(n_core)])

    tied = tie(own, incoming[1], *outgoing[2:])
    own, incoming[1] = tied[:2]
    incoming += [route(places, value) for places, value in zip(ways[2:], tied[2:])]

    def gram(a):
        return lax.dot_general(a, a, (((0,), (0,)), ((), ())), precision=HIGHEST, preferred_element_type=jnp.float32)

    inverse = inverse_factor(gram(own), gram(other))
    inverse, own, other, *incoming = tie(inverse, own, other, *incoming)

    from_z = [z] + [jnp.asarray([places.index(i) for i in range(n_z)])[z] for places in ways]
    order = jnp.stack([core] + [f * n_y + lax.rem(y + k, n_y) for f in from_z for k in range(n_y)]).astype(jnp.int32)
    packed = project(order, own, other, inverse, [piece(z), *incoming])
    packed = packed.astype(jnp.float16).reshape(n_z * n_y, -1, packed.shape[1])
    got = lax.all_to_all(packed, ("z", "y"), split_axis=0, concat_axis=0, tiled=True).astype(jnp.float32)
    got = got[:, :, :n_cols] * jnp.exp2(-got[:, :1, n_cols : n_cols + 1])
    return jnp.transpose(got, (1, 0, 2)).reshape(got.shape[1], -1)


def solution(mesh):
    n_pairs, n_aux = mesh.shape["pairs"], mesh.shape["aux"]
    n_y = 2 ** ((n_pairs.bit_length() - 1) // 2)
    shape = (n_pairs // n_y, n_y, n_aux // 2, 2)
    grid = jax.sharding.Mesh(mesh.devices.reshape(shape), ("z", "y", "x", "core"))
    in_specs = (P(("z", "y"), ("x", "core")), P(("x", "core"), ("z", "y")))
    out_specs = P(("z", "y"), ("x", "core"))
    return jax.shard_map(body, mesh=grid, in_specs=in_specs, out_specs=out_specs, check_vma=False)
```

```python
import jax
import jax.numpy as jnp
from jax import lax
from jax.experimental import pallas as pl
from jax.experimental.layout import Layout, with_layout_constraint
from jax.experimental.pallas import tpu as pltpu
from jax.sharding import PartitionSpec as P

HIGHEST = lax.Precision.HIGHEST


def invert_block(block):
    size = block.shape[0]
    lane = lax.broadcasted_iota(jnp.int32, (8, size), 1)
    sub = lax.broadcasted_iota(jnp.int32, (8, size), 0)

    def across(x, column):
        return jnp.broadcast_to(x[:, column : column + 1], (8, size))

    def down(x, row):
        return jnp.broadcast_to(x[row : row + 1, :], (8, size))

    slabs = [block[8 * i : 8 * i + 8, :] for i in range(size // 8)]
    for g in range(size // 8):
        base = 8 * g
        own = (lane >= base) & (lane < base + 8)
        slab = slabs[g]
        marked = jnp.where(own, jnp.where(lane == sub + base, 1.0, 0.0), slab)
        cols = [across(slab, base + j) for j in range(8)]
        d = {(i, j): down(cols[j], i) for j in range(8) for i in range(j, 8)}
        rows = [down(marked, i) for i in range(8)]
        m, recip = {}, []
        for j in range(8):
            crossed = {(i, k): d[i, j] * d[k, j] for i in range(j + 1, 8) for k in range(j + 1, i + 1)}
            recip.append(1.0 / d[j, j])
            for i in range(j + 1, 8):
                m[i, j] = d[i, j] * recip[j]
            for i in range(j + 1, 8):
                for k in range(j + 1, i + 1):
                    d[i, k] = d[i, k] - crossed[i, k] * recip[j]
                rows[i] = rows[i] - m[i, j] * rows[j]
        solved = [rows[j] * recip[j] for j in range(8)]
        for j in range(6, -1, -1):
            for i in range(7, j, -1):
                solved[j] = solved[j] - m[i, j] * solved[i]
        for i in range(g + 1, size // 8):
            total = jnp.where(own, 0.0, slabs[i])
            for j in range(7, -1, -1):
                total = total - across(slabs[i], base + j) * solved[j]
            slabs[i] = total
        scaled = rows[0] * lax.rsqrt(d[0, 0])
        for j in range(1, 8):
            scaled = jnp.where(sub == j, rows[j] * lax.rsqrt(d[j, j]), scaled)
        slabs[g] = scaled
    return jnp.concatenate(slabs, axis=0)


def eliminate(work, out_ref, strip):
    size = work.shape[0]
    tile = 128
    row_in = lax.broadcasted_iota(jnp.int32, (tile, tile), 0)
    col_in = lax.broadcasted_iota(jnp.int32, (tile, tile), 1)
    col = lax.broadcasted_iota(jnp.int32, (tile, size), 1)

    def step(k, carry):
        at = pl.multiple_of(k * tile, tile)
        here = pl.ds(at, tile)
        inverse = invert_block(work[here, here])
        inverse = jnp.where(row_in >= col_in, inverse, 0.0)
        work[here, here] = jnp.where(row_in == col_in, 1.0, 0.0)
        strip[...] = jnp.dot(inverse, work[here, :], precision=HIGHEST, preferred_element_type=jnp.float32)
        strip[:, here] = inverse
        out_ref[here, :] = jnp.where(col < at + tile, strip[...], 0.0)

        def below(i, carry):
            there = pl.ds(pl.multiple_of(i * tile, tile), tile)
            work[there, here] = jnp.zeros((tile, tile), jnp.float32)
            work[there, :] -= jnp.dot(strip[:, there].T, strip[...], precision=HIGHEST, preferred_element_type=jnp.float32)
            return carry

        return lax.fori_loop(k + 1, size // tile, below, carry)

    lax.fori_loop(0, size // tile, step, 0)


def inverse_factor_kernel(own_ref, other_ref, out_ref, work, strip):
    work[...] = own_ref[...] + other_ref[...]
    eliminate(work, out_ref, strip)


def inverse_factor(own, other):
    size = own.shape[0]
    return pl.pallas_call(
        inverse_factor_kernel,
        out_shape=jax.ShapeDtypeStruct((size, size), jnp.float32),
        in_specs=[pl.BlockSpec(memory_space=pltpu.VMEM)] * 2,
        out_specs=pl.BlockSpec(memory_space=pltpu.VMEM),
        scratch_shapes=[pltpu.VMEM((size, size), jnp.float32), pltpu.VMEM((128, size), jnp.float32)],
        compiler_params=pltpu.CompilerParams(vmem_limit_bytes=24 * 1024 * 1024),
        cost_estimate=pl.CostEstimate(flops=2 * size**3, bytes_accessed=8 * size**2, transcendentals=0),
    )(own, other)


def dot_nt(a, b):
    return lax.dot_general(a, b, (((1,), (1,)), ((), ())), preferred_element_type=jnp.float32)


def two_parts(x):
    high = x.astype(jnp.bfloat16)
    return high, (x - high.astype(jnp.float32)).astype(jnp.bfloat16)


def project_kernel(order_ref, own_ref, other_ref, inverse_ref, *refs):
    *pieces, out_ref, slab_cols, high, middle, w_high, w_middle, product = refs
    _, n_cols, rows = pieces[0].shape
    n_rank, padded = product.shape
    n_own = own_ref.shape[0]
    tile = high.shape[1]
    half = rows // 2

    core = order_ref[0]
    n = 0
    for piece in pieces:
        for j in range(piece.shape[0]):
            n += 1
            at = order_ref[n] * half
            for side, base in ((core, 0), (1 - core, n_own)):
                lanes = pl.ds(pl.multiple_of(side * half, half), half)
                slab_cols[:n_cols, pl.ds(pl.multiple_of(at + base, half), half)] = piece[j, :, lanes]
    if padded > n_cols:
        w_high[n_cols:, :] = jnp.zeros((padded - n_cols, n_rank), jnp.bfloat16)
        w_middle[n_cols:, :] = jnp.zeros((padded - n_cols, n_rank), jnp.bfloat16)

    for top in range(0, n_rank, tile):
        for ref, base in ((own_ref, 0), (other_ref, n_own)):
            parts = two_parts(ref[:, top : top + tile])
            high[base : base + n_own, :], middle[base : base + n_own, :] = parts
        total = jnp.dot(slab_cols[...], middle[...], preferred_element_type=jnp.float32)
        total += jnp.dot(slab_cols[...], high[...], preferred_element_type=jnp.float32)
        w_high[:n_cols, top : top + tile], w_middle[:n_cols, top : top + tile] = two_parts(total)

    largest = jnp.full((1, 1), 1e-30, jnp.float32)
    for top in range(0, n_rank, tile):
        upto = top + tile
        i_high, i_middle = two_parts(inverse_ref[top:upto, :upto])
        value = dot_nt(i_middle, w_high[:, :upto]) + dot_nt(i_high, w_middle[:, :upto])
        value += dot_nt(i_high, w_high[:, :upto])
        product[top:upto, :] = value
        largest = jnp.maximum(largest, jnp.max(jnp.abs(value), keepdims=True))

    power = jnp.floor(14.0 - jnp.log2(largest))
    scale = jnp.exp2(power)
    col = lax.broadcasted_iota(jnp.int32, (tile, padded), 1)
    for top in range(0, n_rank, tile):
        out_ref[top : top + tile, :] = jnp.where(col < n_cols, product[top : top + tile, :] * scale, power)


def project(order, own, other, inverse, pieces):
    _, n_cols, rows = pieces[0].shape
    all_rows, n_rank = 2 * own.shape[0], inverse.shape[0]
    padded = (n_cols // 128 + 1) * 128
    tile = 256
    scratch = [
        ((n_cols, all_rows), jnp.bfloat16),
        ((all_rows, tile), jnp.bfloat16),
        ((all_rows, tile), jnp.bfloat16),
        ((padded, n_rank), jnp.bfloat16),
        ((padded, n_rank), jnp.bfloat16),
        ((n_rank, padded), jnp.float32),
    ]
    held = sum(x.size * x.dtype.itemsize for x in (own, other, inverse, *pieces)) + 4 * n_rank * padded
    held += sum(x[0] * x[1] * jnp.dtype(kind).itemsize for x, kind in scratch)
    return pl.pallas_call(
        project_kernel,
        out_shape=jax.ShapeDtypeStruct((n_rank, padded), jnp.float32),
        in_specs=[pl.BlockSpec(memory_space=pltpu.SMEM)] + [pl.BlockSpec(memory_space=pltpu.VMEM)] * (3 + len(pieces)),
        out_specs=pl.BlockSpec(memory_space=pltpu.VMEM),
        scratch_shapes=[pltpu.VMEM(*x) for x in scratch],
        compiler_params=pltpu.CompilerParams(vmem_limit_bytes=held + 8 * 1024 * 1024),
        cost_estimate=pl.CostEstimate(
            flops=2 * n_cols * n_rank * (2 * all_rows + 2 * n_rank), bytes_accessed=16 * 1024 * 1024, transcendentals=0
        ),
    )(order, own, other, inverse, *pieces)


def rolled(x, start):
    return lax.dynamic_slice_in_dim(jnp.concatenate([x, x], axis=0), start, x.shape[0], axis=0)


def row_major(x):
    return with_layout_constraint(x, Layout(major_to_minor=tuple(range(x.ndim))))


def tie(*arrays):
    return lax.optimization_barrier(arrays)


def routes(n):
    if n == 4:
        return [[2, 0, 3, 1], [1, 3, 0, 2], [3, 2, 1, 0]]
    return [[(i + d) % n for i in range(n)] for d in range(1, n)]


def body(slab, test_matrix):
    z, y, x, core = (lax.axis_index(name) for name in ("z", "y", "x", "core"))
    n_z, n_y, n_x, n_core = (lax.axis_size(name) for name in ("z", "y", "x", "core"))
    n_aux = n_x * n_core
    rows, width = slab.shape[0], test_matrix.shape[1]
    n_cols = slab.shape[1] // (n_z * n_y)

    blocks = [slab] + [
        row_major(lax.ppermute(slab, "y", [((i + k) % n_y, i) for i in range(n_y)])) for k in range(1, n_y)
    ]
    n_aux_rows = test_matrix.shape[0]
    halves = [slice(0, n_aux_rows // 2), slice(n_aux_rows // 2, n_aux_rows)]
    up = [[test_matrix[part].T for part in halves]]
    down = [up[0]]
    for s in range(1, n_z):
        ups = [(i, i + 1) for i in range(s - 1, n_z - 1)]
        downs = [(n_z - 1 - i, n_z - 1 - j) for i, j in ups]
        moved = [(lax.ppermute(u, "z", ups), lax.ppermute(d, "z", downs)) for u, d in zip(up[-1], down[-1])]
        up.append([u for u, _ in moved])
        down.append([d for _, d in moved])
    shards = [(z, up[0])]
    for s in range(1, n_z):
        if 2 * s < n_z:
            shards += [(z - s, up[s]), (z + s, down[s])]
        else:
            shards.append((jnp.where(z >= s, z - s, z + s), [u + d for u, d in zip(up[s], down[s])]))
    turned = [row_major(block.T) for block in blocks]

    def piece(to_z):
        start = (to_z * n_y + y) * n_cols
        return jnp.stack([lax.dynamic_slice(b, (start, 0), (n_cols, rows)) for b in turned])

    def route(places, value):
        return lax.ppermute(value, "z", list(enumerate(places)))

    ways = routes(n_z)
    outgoing = [piece(jnp.asarray(places)[z]) for places in ways]

    def shard_sum(block, some):
        total = 0.0
        for place, shard in some:
            part = sum(jnp.dot(t, block[h], preferred_element_type=jnp.float32) for t, h in zip(shard, halves))
            total += jnp.concatenate([jnp.where(place == i, part, 0.0) for i in range(n_z)], axis=0)
        return total

    early = [shard_sum(block, shards[:-1]) for block in turned]
    place, shard = shards[-1]
    tied = tie(*shard, outgoing[0], *early)
    shard, outgoing[0], early = tied[:2], tied[2], tied[3:]
    incoming = [route(ways[0], outgoing[0])]
    sent = jnp.stack([(e + shard_sum(block, [(place, shard)])).T for e, block in zip(early, turned)])
    sent = rolled(sent, lax.rem(n_y - y, n_y)).reshape(n_y, n_core, n_x, rows // n_aux, n_z * width)

    def exchange(dy, dx, dc):
        part = lax.dynamic_slice(sent, (y ^ dy, core ^ dc, x ^ dx, 0, 0), (1, 1, 1) + sent.shape[3:])[0, 0, 0]
        if dy or dx or dc:
            places = [(i, j, k) for i in range(n_y) for j in range(n_x) for k in range(n_core)]
            pairs = [(n, places.index((i ^ dy, j ^ dx, k ^ dc))) for n, (i, j, k) in enumerate(places)]
            part = lax.ppermute(part, ("y", "x", "core"), pairs)
        return part

    summed = jnp.stack([sum(exchange(dy, dx, dc) for dx in range(n_x) for dc in range(n_core)) for dy in range(n_y)])
    summed = jnp.stack([lax.dynamic_index_in_dim(summed, y ^ k, keepdims=False) for k in range(n_y)])
    summed = jnp.transpose(summed.reshape(n_y, rows // n_aux, n_z, width), (1, 2, 0, 3))
    own_rows = summed.reshape(rows // n_aux, n_z * n_y * width)

    own_rows, incoming[0], near = tie(own_rows, incoming[0], outgoing[1][:1])
    own = lax.all_gather(own_rows, ("z", "y", "x"), axis=0, tiled=True)
    near = route(ways[1], near)

    tied = tie(own, near, outgoing[1][1:], *outgoing[2:])
    own, near, far = tied[:3]
    other = lax.ppermute(own, "core", [(i, n_core - 1 - i) for i in range(n_core)])
    incoming += [near, route(ways[1], far)] + [route(places, value) for places, value in zip(ways[2:], tied[3:])]

    def gram(a):
        return lax.dot_general(a, a, (((0,), (0,)), ((), ())), precision=HIGHEST, preferred_element_type=jnp.float32)

    inverse = inverse_factor(gram(own), gram(other))
    inverse, own, other, *incoming = tie(inverse, own, other, *incoming)

    from_z = [z] + [jnp.asarray([places.index(i) for i in range(n_z)])[z] for places in ways]
    order = jnp.stack([core] + [f * n_y + lax.rem(y + k, n_y) for f in from_z for k in range(n_y)]).astype(jnp.int32)
    packed = project(order, own, other, inverse, [piece(z), *incoming])
    packed = packed.astype(jnp.float16).reshape(n_z * n_y, -1, packed.shape[1])
    got = lax.all_to_all(packed, ("z", "y"), split_axis=0, concat_axis=0, tiled=True).astype(jnp.float32)
    got = got[:, :, :n_cols] * jnp.exp2(-got[:, :1, n_cols : n_cols + 1])
    return jnp.transpose(got, (1, 0, 2)).reshape(got.shape[1], -1)


def solution(mesh):
    n_pairs, n_aux = mesh.shape["pairs"], mesh.shape["aux"]
    n_y = 2 ** ((n_pairs.bit_length() - 1) // 2)
    shape = (n_pairs // n_y, n_y, n_aux // 2, 2)
    grid = jax.sharding.Mesh(mesh.devices.reshape(shape), ("z", "y", "x", "core"))
    in_specs = (P(("z", "y"), ("x", "core")), P(("x", "core"), ("z", "y")))
    out_specs = P(("z", "y"), ("x", "core"))
    return jax.shard_map(body, mesh=grid, in_specs=in_specs, out_specs=out_specs, check_vma=False)
```

```python
import jax
import jax.numpy as jnp
from jax import lax
from jax.experimental import pallas as pl
from jax.experimental.layout import Layout, with_layout_constraint
from jax.experimental.pallas import tpu as pltpu
from jax.sharding import PartitionSpec as P

HIGHEST = lax.Precision.HIGHEST


def invert_block(block):
    size = block.shape[0]
    lane = lax.broadcasted_iota(jnp.int32, (8, size), 1)
    sub = lax.broadcasted_iota(jnp.int32, (8, size), 0)

    def across(x, column):
        return jnp.broadcast_to(x[:, column : column + 1], (8, size))

    def down(x, row):
        return jnp.broadcast_to(x[row : row + 1, :], (8, size))

    slabs = [block[8 * i : 8 * i + 8, :] for i in range(size // 8)]
    for g in range(size // 8):
        base = 8 * g
        own = (lane >= base) & (lane < base + 8)
        slab = slabs[g]
        marked = jnp.where(own, jnp.where(lane == sub + base, 1.0, 0.0), slab)
        cols = [across(slab, base + j) for j in range(8)]
        d = {(i, j): down(cols[j], i) for j in range(8) for i in range(j, 8)}
        rows = [down(marked, i) for i in range(8)]
        m, recip = {}, []
        for j in range(8):
            crossed = {(i, k): d[i, j] * d[k, j] for i in range(j + 1, 8) for k in range(j + 1, i + 1)}
            recip.append(1.0 / d[j, j])
            for i in range(j + 1, 8):
                m[i, j] = d[i, j] * recip[j]
            for i in range(j + 1, 8):
                for k in range(j + 1, i + 1):
                    d[i, k] = d[i, k] - crossed[i, k] * recip[j]
                rows[i] = rows[i] - m[i, j] * rows[j]
        solved = [rows[j] * recip[j] for j in range(8)]
        for j in range(6, -1, -1):
            for i in range(7, j, -1):
                solved[j] = solved[j] - m[i, j] * solved[i]
        for i in range(g + 1, size // 8):
            total = jnp.where(own, 0.0, slabs[i])
            for j in range(7, -1, -1):
                total = total - across(slabs[i], base + j) * solved[j]
            slabs[i] = total
        scaled = rows[0] * lax.rsqrt(d[0, 0])
        for j in range(1, 8):
            scaled = jnp.where(sub == j, rows[j] * lax.rsqrt(d[j, j]), scaled)
        slabs[g] = scaled
    return jnp.concatenate(slabs, axis=0)


def eliminate(work, out_ref, strip):
    size = work.shape[0]
    tile = 128
    row_in = lax.broadcasted_iota(jnp.int32, (tile, tile), 0)
    col_in = lax.broadcasted_iota(jnp.int32, (tile, tile), 1)
    col = lax.broadcasted_iota(jnp.int32, (tile, size), 1)

    def step(k, carry):
        at = pl.multiple_of(k * tile, tile)
        here = pl.ds(at, tile)
        inverse = invert_block(work[here, here])
        inverse = jnp.where(row_in >= col_in, inverse, 0.0)
        work[here, here] = jnp.where(row_in == col_in, 1.0, 0.0)
        strip[...] = jnp.dot(inverse, work[here, :], precision=HIGHEST, preferred_element_type=jnp.float32)
        strip[:, here] = inverse
        out_ref[here, :] = jnp.where(col < at + tile, strip[...], 0.0)

        def below(i, carry):
            there = pl.ds(pl.multiple_of(i * tile, tile), tile)
            work[there, here] = jnp.zeros((tile, tile), jnp.float32)
            work[there, :] -= jnp.dot(strip[:, there].T, strip[...], precision=HIGHEST, preferred_element_type=jnp.float32)
            return carry

        return lax.fori_loop(k + 1, size // tile, below, carry)

    lax.fori_loop(0, size // tile, step, 0)


def inverse_factor_kernel(own_ref, other_ref, out_ref, work, strip):
    work[...] = own_ref[...] + other_ref[...]
    eliminate(work, out_ref, strip)


def inverse_factor(own, other):
    size = own.shape[0]
    return pl.pallas_call(
        inverse_factor_kernel,
        out_shape=jax.ShapeDtypeStruct((size, size), jnp.float32),
        in_specs=[pl.BlockSpec(memory_space=pltpu.VMEM)] * 2,
        out_specs=pl.BlockSpec(memory_space=pltpu.VMEM),
        scratch_shapes=[pltpu.VMEM((size, size), jnp.float32), pltpu.VMEM((128, size), jnp.float32)],
        compiler_params=pltpu.CompilerParams(vmem_limit_bytes=24 * 1024 * 1024),
        cost_estimate=pl.CostEstimate(flops=2 * size**3, bytes_accessed=8 * size**2, transcendentals=0),
    )(own, other)


def dot_nt(a, b):
    return lax.dot_general(a, b, (((1,), (1,)), ((), ())), preferred_element_type=jnp.float32)


def two_parts(x):
    high = x.astype(jnp.bfloat16)
    return high, (x - high.astype(jnp.float32)).astype(jnp.bfloat16)


def project_kernel(order_ref, own_ref, other_ref, inverse_ref, *refs):
    *pieces, out_ref, slab_cols, high, middle, w_high, w_middle, product = refs
    _, n_cols, rows = pieces[0].shape
    n_rank, padded = product.shape
    n_own = own_ref.shape[0]
    tile = high.shape[1]
    half = rows // 2

    core = order_ref[0]
    n = 0
    for piece in pieces:
        for j in range(piece.shape[0]):
            n += 1
            at = order_ref[n] * half
            for side, base in ((core, 0), (1 - core, n_own)):
                lanes = pl.ds(pl.multiple_of(side * half, half), half)
                slab_cols[:n_cols, pl.ds(pl.multiple_of(at + base, half), half)] = piece[j, :, lanes]
    if padded > n_cols:
        w_high[n_cols:, :] = jnp.zeros((padded - n_cols, n_rank), jnp.bfloat16)
        w_middle[n_cols:, :] = jnp.zeros((padded - n_cols, n_rank), jnp.bfloat16)

    for top in range(0, n_rank, tile):
        for ref, base in ((own_ref, 0), (other_ref, n_own)):
            parts = two_parts(ref[:, top : top + tile])
            high[base : base + n_own, :], middle[base : base + n_own, :] = parts
        total = jnp.dot(slab_cols[...], middle[...], preferred_element_type=jnp.float32)
        total += jnp.dot(slab_cols[...], high[...], preferred_element_type=jnp.float32)
        w_high[:n_cols, top : top + tile], w_middle[:n_cols, top : top + tile] = two_parts(total)

    largest = jnp.full((1, 1), 1e-30, jnp.float32)
    for top in range(0, n_rank, tile):
        upto = top + tile
        i_high, i_middle = two_parts(inverse_ref[top:upto, :upto])
        value = dot_nt(i_middle, w_high[:, :upto]) + dot_nt(i_high, w_middle[:, :upto])
        value += dot_nt(i_high, w_high[:, :upto])
        product[top:upto, :] = value
        largest = jnp.maximum(largest, jnp.max(jnp.abs(value), keepdims=True))

    power = jnp.floor(14.0 - jnp.log2(largest))
    scale = jnp.exp2(power)
    col = lax.broadcasted_iota(jnp.int32, (tile, padded), 1)
    for top in range(0, n_rank, tile):
        out_ref[top : top + tile, :] = jnp.where(col < n_cols, product[top : top + tile, :] * scale, power)


def project(order, own, other, inverse, pieces):
    _, n_cols, rows = pieces[0].shape
    all_rows, n_rank = 2 * own.shape[0], inverse.shape[0]
    padded = (n_cols // 128 + 1) * 128
    tile = 256
    scratch = [
        ((n_cols, all_rows), jnp.bfloat16),
        ((all_rows, tile), jnp.bfloat16),
        ((all_rows, tile), jnp.bfloat16),
        ((padded, n_rank), jnp.bfloat16),
        ((padded, n_rank), jnp.bfloat16),
        ((n_rank, padded), jnp.float32),
    ]
    held = sum(x.size * x.dtype.itemsize for x in (own, other, inverse, *pieces)) + 4 * n_rank * padded
    held += sum(x[0] * x[1] * jnp.dtype(kind).itemsize for x, kind in scratch)
    return pl.pallas_call(
        project_kernel,
        out_shape=jax.ShapeDtypeStruct((n_rank, padded), jnp.float32),
        in_specs=[pl.BlockSpec(memory_space=pltpu.SMEM)] + [pl.BlockSpec(memory_space=pltpu.VMEM)] * (3 + len(pieces)),
        out_specs=pl.BlockSpec(memory_space=pltpu.VMEM),
        scratch_shapes=[pltpu.VMEM(*x) for x in scratch],
        compiler_params=pltpu.CompilerParams(vmem_limit_bytes=held + 8 * 1024 * 1024),
        cost_estimate=pl.CostEstimate(
            flops=2 * n_cols * n_rank * (2 * all_rows + 2 * n_rank), bytes_accessed=16 * 1024 * 1024, transcendentals=0
        ),
    )(order, own, other, inverse, *pieces)


def rolled(x, start):
    return lax.dynamic_slice_in_dim(jnp.concatenate([x, x], axis=0), start, x.shape[0], axis=0)


def row_major(x):
    return with_layout_constraint(x, Layout(major_to_minor=tuple(range(x.ndim))))


def tie(*arrays):
    return lax.optimization_barrier(arrays)


def routes(n):
    if n == 4:
        return [[2, 0, 3, 1], [1, 3, 0, 2], [3, 2, 1, 0]]
    return [[(i + d) % n for i in range(n)] for d in range(1, n)]


def body(slab, test_matrix):
    z, y, x, core = (lax.axis_index(name) for name in ("z", "y", "x", "core"))
    n_z, n_y, n_x, n_core = (lax.axis_size(name) for name in ("z", "y", "x", "core"))
    n_aux = n_x * n_core
    rows, width = slab.shape[0], test_matrix.shape[1]
    n_cols = slab.shape[1] // (n_z * n_y)

    blocks = [slab] + [
        row_major(lax.ppermute(slab, "y", [((i + k) % n_y, i) for i in range(n_y)])) for k in range(1, n_y)
    ]
    up = [test_matrix.T]
    down = [up[0]]
    for s in range(1, n_z):
        up.append(lax.ppermute(up[-1], "z", [(i, i + 1) for i in range(s - 1, n_z - 1)]))
        down.append(lax.ppermute(down[-1], "z", [(i + 1, i) for i in range(n_z - s)]))
    shards = [(z, up[0])]
    for s in range(1, n_z):
        if 2 * s < n_z:
            shards += [(z - s, up[s]), (z + s, down[s])]
        else:
            shards.append((jnp.where(z >= s, z - s, z + s), up[s] + down[s]))

    turned = [row_major(block.T) for block in blocks]

    def shard_sum(block):
        total = 0.0
        for place, shard in shards:
            part = jnp.dot(shard, block, preferred_element_type=jnp.float32)
            total += jnp.concatenate([jnp.where(place == i, part, 0.0) for i in range(n_z)], axis=0)
        return total.T

    sent = jnp.stack([shard_sum(block) for block in turned])
    sent = rolled(sent, lax.rem(n_y - y, n_y)).reshape(n_y, n_core, n_x, rows // n_aux, n_z * width)

    def piece(to_z):
        start = (to_z * n_y + y) * n_cols
        return jnp.stack([lax.dynamic_slice(b, (start, 0), (n_cols, rows)) for b in turned])

    def route(places, value):
        return lax.ppermute(value, "z", list(enumerate(places)))

    ways = routes(n_z)
    outgoing = [piece(jnp.asarray(places)[z]) for places in ways]
    outgoing[0], up[-1], down[-1] = tie(outgoing[0], up[-1], down[-1])
    incoming = [route(ways[0], outgoing[0])]

    def exchange(dy, dx, dc):
        part = lax.dynamic_slice(sent, (y ^ dy, core ^ dc, x ^ dx, 0, 0), (1, 1, 1) + sent.shape[3:])[0, 0, 0]
        if dy or dx or dc:
            places = [(i, j, k) for i in range(n_y) for j in range(n_x) for k in range(n_core)]
            pairs = [(n, places.index((i ^ dy, j ^ dx, k ^ dc))) for n, (i, j, k) in enumerate(places)]
            part = lax.ppermute(part, ("y", "x", "core"), pairs)
        return part

    summed = jnp.stack([sum(exchange(dy, dx, dc) for dx in range(n_x) for dc in range(n_core)) for dy in range(n_y)])
    summed = jnp.stack([lax.dynamic_index_in_dim(summed, y ^ k, keepdims=False) for k in range(n_y)])
    summed = jnp.transpose(summed.reshape(n_y, rows // n_aux, n_z, width), (1, 2, 0, 3))
    own_rows = summed.reshape(rows // n_aux, n_z * n_y * width)

    own_rows, incoming[0], near = tie(own_rows, incoming[0], outgoing[1][:1])
    own = lax.all_gather(own_rows, ("z", "y", "x"), axis=0, tiled=True)
    near = route(ways[1], near)

    tied = tie(own, near, outgoing[1][1:], *outgoing[2:])
    own, near, far = tied[:3]
    other = lax.ppermute(own, "core", [(i, n_core - 1 - i) for i in range(n_core)])
    incoming += [near, route(ways[1], far)] + [route(places, value) for places, value in zip(ways[2:], tied[3:])]

    def gram(a):
        return lax.dot_general(a, a, (((0,), (0,)), ((), ())), precision=HIGHEST, preferred_element_type=jnp.float32)

    inverse = inverse_factor(gram(own), gram(other))
    inverse, own, other, *incoming = tie(inverse, own, other, *incoming)

    from_z = [z] + [jnp.asarray([places.index(i) for i in range(n_z)])[z] for places in ways]
    order = jnp.stack([core] + [f * n_y + lax.rem(y + k, n_y) for f in from_z for k in range(n_y)]).astype(jnp.int32)
    packed = project(order, own, other, inverse, [piece(z), *incoming])
    packed = packed.astype(jnp.float16).reshape(n_z * n_y, -1, packed.shape[1])
    got = lax.all_to_all(packed, ("z", "y"), split_axis=0, concat_axis=0, tiled=True).astype(jnp.float32)
    got = got[:, :, :n_cols] * jnp.exp2(-got[:, :1, n_cols : n_cols + 1])
    return jnp.transpose(got, (1, 0, 2)).reshape(got.shape[1], -1)


def solution(mesh):
    n_pairs, n_aux = mesh.shape["pairs"], mesh.shape["aux"]
    n_y = 2 ** ((n_pairs.bit_length() - 1) // 2)
    shape = (n_pairs // n_y, n_y, n_aux // 2, 2)
    grid = jax.sharding.Mesh(mesh.devices.reshape(shape), ("z", "y", "x", "core"))
    in_specs = (P(("z", "y"), ("x", "core")), P(("x", "core"), ("z", "y")))
    out_specs = P(("z", "y"), ("x", "core"))
    return jax.shard_map(body, mesh=grid, in_specs=in_specs, out_specs=out_specs, check_vma=False)
```

```python
import jax
import jax.numpy as jnp
from jax import lax
from jax.experimental import pallas as pl
from jax.experimental.layout import Layout, with_layout_constraint
from jax.experimental.pallas import tpu as pltpu
from jax.sharding import PartitionSpec as P

HIGHEST = lax.Precision.HIGHEST


def invert_block(block):
    size = block.shape[0]
    lane = lax.broadcasted_iota(jnp.int32, (8, size), 1)
    sub = lax.broadcasted_iota(jnp.int32, (8, size), 0)

    def across(x, column):
        return jnp.broadcast_to(x[:, column : column + 1], (8, size))

    def down(x, row):
        return jnp.broadcast_to(x[row : row + 1, :], (8, size))

    slabs = [block[8 * i : 8 * i + 8, :] for i in range(size // 8)]
    for g in range(size // 8):
        base = 8 * g
        own = (lane >= base) & (lane < base + 8)
        slab = slabs[g]
        marked = jnp.where(own, jnp.where(lane == sub + base, 1.0, 0.0), slab)
        cols = [across(slab, base + j) for j in range(8)]
        d = {(i, j): down(cols[j], i) for j in range(8) for i in range(j, 8)}
        rows = [down(marked, i) for i in range(8)]
        m, recip = {}, []
        for j in range(8):
            crossed = {(i, k): d[i, j] * d[k, j] for i in range(j + 1, 8) for k in range(j + 1, i + 1)}
            recip.append(1.0 / d[j, j])
            for i in range(j + 1, 8):
                m[i, j] = d[i, j] * recip[j]
            for i in range(j + 1, 8):
                for k in range(j + 1, i + 1):
                    d[i, k] = d[i, k] - crossed[i, k] * recip[j]
                rows[i] = rows[i] - m[i, j] * rows[j]
        solved = [rows[j] * recip[j] for j in range(8)]
        for j in range(6, -1, -1):
            for i in range(7, j, -1):
                solved[j] = solved[j] - m[i, j] * solved[i]
        for i in range(g + 1, size // 8):
            total = jnp.where(own, 0.0, slabs[i])
            for j in range(7, -1, -1):
                total = total - across(slabs[i], base + j) * solved[j]
            slabs[i] = total
        scaled = rows[0] * lax.rsqrt(d[0, 0])
        for j in range(1, 8):
            scaled = jnp.where(sub == j, rows[j] * lax.rsqrt(d[j, j]), scaled)
        slabs[g] = scaled
    return jnp.concatenate(slabs, axis=0)


def eliminate(work, out_ref, strip):
    size = work.shape[0]
    tile = 128
    row_in = lax.broadcasted_iota(jnp.int32, (tile, tile), 0)
    col_in = lax.broadcasted_iota(jnp.int32, (tile, tile), 1)
    col = lax.broadcasted_iota(jnp.int32, (tile, size), 1)
    chunk = 2 * tile
    row_at = lax.broadcasted_iota(jnp.int32, (chunk, tile), 0)

    def step(k, carry):
        at = pl.multiple_of(k * tile, tile)
        here = pl.ds(at, tile)
        inverse = invert_block(work[here, here])
        inverse = jnp.where(row_in >= col_in, inverse, 0.0)
        work[here, here] = jnp.where(row_in == col_in, 1.0, 0.0)
        strip[...] = jnp.dot(inverse, work[here, :], precision=HIGHEST, preferred_element_type=jnp.float32)
        strip[:, here] = inverse
        out_ref[here, :] = jnp.where(col < at + tile, strip[...], 0.0)

        def below(i, carry):
            start = pl.multiple_of(i * chunk, chunk)
            there = pl.ds(start, chunk)
            under = row_at >= at + tile - start
            work[there, here] = jnp.where(under, 0.0, work[there, here])
            lower = jnp.where(under, strip[:, there].T, 0.0)
            work[there, :] -= jnp.dot(lower, strip[...], precision=HIGHEST, preferred_element_type=jnp.float32)
            return carry

        return lax.fori_loop((at + tile) // chunk, size // chunk, below, carry)

    lax.fori_loop(0, size // tile, step, 0)


def inverse_factor_kernel(own_ref, other_ref, out_ref, work, strip):
    work[...] = own_ref[...] + other_ref[...]
    eliminate(work, out_ref, strip)


def inverse_factor(own, other):
    size = own.shape[0]
    return pl.pallas_call(
        inverse_factor_kernel,
        out_shape=jax.ShapeDtypeStruct((size, size), jnp.float32),
        in_specs=[pl.BlockSpec(memory_space=pltpu.VMEM)] * 2,
        out_specs=pl.BlockSpec(memory_space=pltpu.VMEM),
        scratch_shapes=[pltpu.VMEM((size, size), jnp.float32), pltpu.VMEM((128, size), jnp.float32)],
        compiler_params=pltpu.CompilerParams(vmem_limit_bytes=24 * 1024 * 1024),
        cost_estimate=pl.CostEstimate(flops=2 * size**3, bytes_accessed=8 * size**2, transcendentals=0),
    )(own, other)


def dot_nt(a, b):
    return lax.dot_general(a, b, (((1,), (1,)), ((), ())), preferred_element_type=jnp.float32)


def two_parts(x):
    high = x.astype(jnp.bfloat16)
    return high, (x - high.astype(jnp.float32)).astype(jnp.bfloat16)


def project_kernel(order_ref, own_ref, other_ref, inverse_ref, *refs):
    *pieces, out_ref, slab_cols, high, middle, w_high, w_middle, product = refs
    _, n_cols, rows = pieces[0].shape
    n_rank, padded = product.shape
    n_own = own_ref.shape[0]
    tile = high.shape[1]
    half = rows // 2

    core = order_ref[0]
    n = 0
    for piece in pieces:
        for j in range(piece.shape[0]):
            n += 1
            at = order_ref[n] * half
            for side, base in ((core, 0), (1 - core, n_own)):
                lanes = pl.ds(pl.multiple_of(side * half, half), half)
                slab_cols[:n_cols, pl.ds(pl.multiple_of(at + base, half), half)] = piece[j, :, lanes]
    if padded > n_cols:
        w_high[n_cols:, :] = jnp.zeros((padded - n_cols, n_rank), jnp.bfloat16)
        w_middle[n_cols:, :] = jnp.zeros((padded - n_cols, n_rank), jnp.bfloat16)

    for top in range(0, n_rank, tile):
        for ref, base in ((own_ref, 0), (other_ref, n_own)):
            parts = two_parts(ref[:, top : top + tile])
            high[base : base + n_own, :], middle[base : base + n_own, :] = parts
        total = jnp.dot(slab_cols[...], middle[...], preferred_element_type=jnp.float32)
        total += jnp.dot(slab_cols[...], high[...], preferred_element_type=jnp.float32)
        w_high[:n_cols, top : top + tile], w_middle[:n_cols, top : top + tile] = two_parts(total)

    largest = jnp.full((1, 1), 1e-30, jnp.float32)
    for top in range(0, n_rank, tile):
        upto = top + tile
        i_high, i_middle = two_parts(inverse_ref[top:upto, :upto])
        value = dot_nt(i_middle, w_high[:, :upto]) + dot_nt(i_high, w_middle[:, :upto])
        value += dot_nt(i_high, w_high[:, :upto])
        product[top:upto, :] = value
        largest = jnp.maximum(largest, jnp.max(jnp.abs(value), keepdims=True))

    power = jnp.floor(14.0 - jnp.log2(largest))
    scale = jnp.exp2(power)
    col = lax.broadcasted_iota(jnp.int32, (tile, padded), 1)
    for top in range(0, n_rank, tile):
        out_ref[top : top + tile, :] = jnp.where(col < n_cols, product[top : top + tile, :] * scale, power)


def project(order, own, other, inverse, pieces):
    _, n_cols, rows = pieces[0].shape
    all_rows, n_rank = 2 * own.shape[0], inverse.shape[0]
    padded = (n_cols // 128 + 1) * 128
    tile = 256
    scratch = [
        ((n_cols, all_rows), jnp.bfloat16),
        ((all_rows, tile), jnp.bfloat16),
        ((all_rows, tile), jnp.bfloat16),
        ((padded, n_rank), jnp.bfloat16),
        ((padded, n_rank), jnp.bfloat16),
        ((n_rank, padded), jnp.float32),
    ]
    held = sum(x.size * x.dtype.itemsize for x in (own, other, inverse, *pieces)) + 4 * n_rank * padded
    held += sum(x[0] * x[1] * jnp.dtype(kind).itemsize for x, kind in scratch)
    return pl.pallas_call(
        project_kernel,
        out_shape=jax.ShapeDtypeStruct((n_rank, padded), jnp.float32),
        in_specs=[pl.BlockSpec(memory_space=pltpu.SMEM)] + [pl.BlockSpec(memory_space=pltpu.VMEM)] * (3 + len(pieces)),
        out_specs=pl.BlockSpec(memory_space=pltpu.VMEM),
        scratch_shapes=[pltpu.VMEM(*x) for x in scratch],
        compiler_params=pltpu.CompilerParams(vmem_limit_bytes=held + 8 * 1024 * 1024),
        cost_estimate=pl.CostEstimate(
            flops=2 * n_cols * n_rank * (2 * all_rows + 2 * n_rank), bytes_accessed=16 * 1024 * 1024, transcendentals=0
        ),
    )(order, own, other, inverse, *pieces)


def rolled(x, start):
    return lax.dynamic_slice_in_dim(jnp.concatenate([x, x], axis=0), start, x.shape[0], axis=0)


def row_major(x):
    return with_layout_constraint(x, Layout(major_to_minor=tuple(range(x.ndim))))


def tie(*arrays):
    return lax.optimization_barrier(arrays)


def routes(n):
    if n == 4:
        return [[2, 0, 3, 1], [1, 3, 0, 2], [3, 2, 1, 0]]
    return [[(i + d) % n for i in range(n)] for d in range(1, n)]


def body(slab, test_matrix):
    z, y, x, core = (lax.axis_index(name) for name in ("z", "y", "x", "core"))
    n_z, n_y, n_x, n_core = (lax.axis_size(name) for name in ("z", "y", "x", "core"))
    n_aux = n_x * n_core
    rows, width = slab.shape[0], test_matrix.shape[1]
    n_cols = slab.shape[1] // (n_z * n_y)

    blocks = [slab] + [
        row_major(lax.ppermute(slab, "y", [((i + k) % n_y, i) for i in range(n_y)])) for k in range(1, n_y)
    ]
    up = [test_matrix.T]
    down = [up[0]]
    for s in range(1, n_z):
        up.append(lax.ppermute(up[-1], "z", [(i, i + 1) for i in range(s - 1, n_z - 1)]))
        down.append(lax.ppermute(down[-1], "z", [(i + 1, i) for i in range(n_z - s)]))
    shards = [(z, up[0])]
    for s in range(1, n_z):
        if 2 * s < n_z:
            shards += [(z - s, up[s]), (z + s, down[s])]
        else:
            shards.append((jnp.where(z >= s, z - s, z + s), up[s] + down[s]))

    turned = [row_major(block.T) for block in blocks]

    def shard_sum(block):
        total = 0.0
        for place, shard in shards:
            part = jnp.dot(shard, block, preferred_element_type=jnp.float32)
            total += jnp.concatenate([jnp.where(place == i, part, 0.0) for i in range(n_z)], axis=0)
        return total.T

    sent = jnp.stack([shard_sum(block) for block in turned])
    sent = rolled(sent, lax.rem(n_y - y, n_y)).reshape(n_y, n_core, n_x, rows // n_aux, n_z * width)

    def piece(to_z):
        start = (to_z * n_y + y) * n_cols
        return jnp.stack([lax.dynamic_slice(b, (start, 0), (n_cols, rows)) for b in turned])

    def route(places, value):
        return lax.ppermute(value, "z", list(enumerate(places)))

    ways = routes(n_z)
    outgoing = [piece(jnp.asarray(places)[z]) for places in ways]
    outgoing[0], up[-1], down[-1] = tie(outgoing[0], up[-1], down[-1])
    incoming = [route(ways[0], outgoing[0])]

    def exchange(dy, dx, dc):
        part = lax.dynamic_slice(sent, (y ^ dy, core ^ dc, x ^ dx, 0, 0), (1, 1, 1) + sent.shape[3:])[0, 0, 0]
        if dy or dx or dc:
            places = [(i, j, k) for i in range(n_y) for j in range(n_x) for k in range(n_core)]
            pairs = [(n, places.index((i ^ dy, j ^ dx, k ^ dc))) for n, (i, j, k) in enumerate(places)]
            part = lax.ppermute(part, ("y", "x", "core"), pairs)
        return part

    summed = jnp.stack([sum(exchange(dy, dx, dc) for dx in range(n_x) for dc in range(n_core)) for dy in range(n_y)])
    summed = jnp.stack([lax.dynamic_index_in_dim(summed, y ^ k, keepdims=False) for k in range(n_y)])
    summed = jnp.transpose(summed.reshape(n_y, rows // n_aux, n_z, width), (1, 2, 0, 3))
    own_rows = summed.reshape(rows // n_aux, n_z * n_y * width)

    own_rows, incoming[0], near = tie(own_rows, incoming[0], outgoing[1][:1])
    own = lax.all_gather(own_rows, ("z", "y", "x"), axis=0, tiled=True)
    near = route(ways[1], near)

    tied = tie(own, near, outgoing[1][1:], *outgoing[2:])
    own, near, far = tied[:3]
    other = lax.ppermute(own, "core", [(i, n_core - 1 - i) for i in range(n_core)])
    incoming += [near, route(ways[1], far)] + [route(places, value) for places, value in zip(ways[2:], tied[3:])]

    def gram(a):
        return lax.dot_general(a, a, (((0,), (0,)), ((), ())), precision=HIGHEST, preferred_element_type=jnp.float32)

    inverse = inverse_factor(gram(own), gram(other))
    inverse, own, other, *incoming = tie(inverse, own, other, *incoming)

    from_z = [z] + [jnp.asarray([places.index(i) for i in range(n_z)])[z] for places in ways]
    order = jnp.stack([core] + [f * n_y + lax.rem(y + k, n_y) for f in from_z for k in range(n_y)]).astype(jnp.int32)
    packed = project(order, own, other, inverse, [piece(z), *incoming])
    packed = packed.astype(jnp.float16).reshape(n_z * n_y, -1, packed.shape[1])
    got = lax.all_to_all(packed, ("z", "y"), split_axis=0, concat_axis=0, tiled=True).astype(jnp.float32)
    got = got[:, :, :n_cols] * jnp.exp2(-got[:, :1, n_cols : n_cols + 1])
    return jnp.transpose(got, (1, 0, 2)).reshape(got.shape[1], -1)


def solution(mesh):
    n_pairs, n_aux = mesh.shape["pairs"], mesh.shape["aux"]
    n_y = 2 ** ((n_pairs.bit_length() - 1) // 2)
    shape = (n_pairs // n_y, n_y, n_aux // 2, 2)
    grid = jax.sharding.Mesh(mesh.devices.reshape(shape), ("z", "y", "x", "core"))
    in_specs = (P(("z", "y"), ("x", "core")), P(("x", "core"), ("z", "y")))
    out_specs = P(("z", "y"), ("x", "core"))
    return jax.shard_map(body, mesh=grid, in_specs=in_specs, out_specs=out_specs, check_vma=False)
```
